32 devices in a mesh: item: 8 (over y, x, core), user: 4 (over z).
Axes of the slice: x: 2, y: 2, z: 4, core: 2. Of those that a mesh axis runs over, the one named last changes fastest.
Arguments:
- user_factors: bfloat16 [32256, 128], P(('user', 'item')), may hold values from -0.13 to 0.13
- ratings: bfloat16 [224, 32, 128], P('user', 'item'), may hold values from 0.049804688 to 5
- block_owner: int32 [8, 224], P('item', 'user'), may hold values from 0 to 3, as said below
- owner_block_position: int32 [8, 224], P('item', 'user'), may hold values from 0 to 62
- block_count: int32 [8, 4], P('item', 'user'), may hold values from 14 to 56, as said below
Outputs:
- item_factors: float32 [32, 128], P(('item', 'user'))
The draws below stay inside these ranges and needn't reach their ends.
Inputs may be any that keep to these rules, and one draw needn't show every extreme that they name: `block_owner`: among the 56 blocks of one device no index of user is named more than 21 times; on every index of item one index of user is named exactly 21 times by the blocks of every index of user. `block_count`: on every index of item exactly one index of user holds 56 live blocks, the others 56 // 4 to 28; the live blocks are the first slots.
All inputs are finite; a program needn't handle non-finite values.
Results may differ from the reference program's by a relative error of at most 0.0003.
Values may be sent and summed in bfloat16 or wider, within the bound.
A program may use at most 64 MiB of HBM per device.

```python
import math
import jax
import jax.numpy as jnp
from jax import lax

K = 128
BU = 128
NB_CAP = 56
ITERS = 8
CAP = 21
UB_DEV = 63
USERS = 32256
ITEMS_DEV = 4
ITEMS = 32
N_ITEM = 8
N_USER = 4


def draw_user_factors(key, part):
    key_scale, key_base = jax.random.split(key, 2)
    column_scale = jnp.exp(jax.random.uniform(key_scale, (1, K), minval=math.log(0.002), maxval=math.log(0.02)))
    base = jnp.clip(jax.random.normal(key_base, (USERS, K)), -4.0, 4.0)
    mixed = base + 0.5 * jnp.roll(base, 1, axis=1)
    return (mixed * column_scale).astype(jnp.float32).astype(jnp.bfloat16)


def draw_block_owner(key, part):
    key_heavy, key_pick, key_order = jax.random.split(key, 3)
    places = N_USER * CAP
    heavy = jax.random.randint(key_heavy, (N_ITEM, 1, 1), 0, N_USER)
    spots = jnp.arange(places, dtype=jnp.int32)
    noise = jax.random.randint(key_pick, (N_ITEM, N_USER, places), 0, 4096) * places + spots
    scores = jnp.where(spots < CAP, spots - places, noise)
    chosen = jnp.argsort(scores, axis=-1)[:, :, :NB_CAP].astype(jnp.int32)
    shuffle = jax.random.randint(key_order, (N_ITEM, N_USER, NB_CAP), 0, 4096) * NB_CAP + jnp.arange(NB_CAP, dtype=jnp.int32)
    ranking = jnp.argsort(shuffle, axis=-1)
    chosen = jnp.take_along_axis(chosen, ranking, axis=-1)
    owners = (chosen // CAP + heavy) % N_USER
    return owners.reshape(N_ITEM, N_USER * NB_CAP).astype(jnp.int32)


def draw_block_count(key, part):
    key_base, key_heavy = jax.random.split(key, 2)
    base = jax.random.randint(key_base, (N_ITEM, N_USER), NB_CAP // 4, NB_CAP // 2 + 1)
    heavy = jax.random.randint(key_heavy, (N_ITEM, 1), 0, N_USER)
    filled = jnp.where(jnp.arange(N_USER, dtype=jnp.int32)[None, :] == heavy, NB_CAP, base)
    return filled.astype(jnp.int32)


def with_ends(values, own_key, least, high):
    shape = values.shape
    place = [jax.random.randint(jax.random.fold_in(own_key, axis), (), 0, shape[axis]) for axis in range(len(shape))]
    values = values.at[tuple(place)].set(least)
    longest = shape.index(max(shape))
    place[longest] = (place[longest] + 1) % shape[longest]
    return values.at[tuple(place)].set(high)


def block_scale(stream_key, shape, pieces, low, largest):
    factor_of = 1.0
    for axis_at, shards_of in pieces:
        draws = jax.random.uniform(jax.random.fold_in(jax.random.fold_in(stream_key, 6), axis_at), (shards_of,), jnp.float32, low / len(pieces), largest / len(pieces))
        factor_of = factor_of * jnp.repeat(jnp.exp(draws), shape[axis_at] // shards_of).reshape((-1,) + (1,) * (len(shape) - 1 - axis_at))
    return factor_of


def setup_inputs(seed: int = 0) -> dict:
    seeds = jax.random.split(jax.random.key(seed), 6)
    return {
        "user_factors": draw_user_factors(jax.random.fold_in(seeds[5], 71), 0),
        "ratings": jnp.clip(jnp.exp(math.log(5.0) - 4.609084 * jax.random.uniform(seeds[1], (N_USER * NB_CAP, ITEMS, BU), jnp.float32) ** block_scale(seeds[1], (N_USER * NB_CAP, ITEMS, BU), ((0, 4), (1, 8)), -0.2, 0.2)), 0.049804688, 5.0).astype(jnp.bfloat16),
        "block_owner": draw_block_owner(jax.random.fold_in(seeds[5], 71), 0),
        "owner_block_position": with_ends(jax.random.randint(seeds[3], (N_ITEM, N_USER * NB_CAP), 0, UB_DEV), jax.random.fold_in(seeds[3], 1), 0, UB_DEV - 1).astype(jnp.int32),
        "block_count": draw_block_count(jax.random.fold_in(seeds[5], 71), 0),
    }


ridge_weight = 0.05
small_eps = 1e-6
members_per_group = 8


def conjugate_solve(system, right_side):
    solution = jnp.zeros_like(right_side)
    residual = right_side
    direction = right_side
    norm_now = jnp.sum(residual * residual, axis=-1, keepdims=True)
    for iteration in range(ITERS):
        image = jnp.einsum('jkl,jl->jk', system, direction, precision=lax.Precision.HIGHEST)
        alpha = norm_now / (jnp.sum(direction * image, axis=-1, keepdims=True) + small_eps)
        solution = solution + alpha * direction
        residual = residual - alpha * image
        norm_next = jnp.sum(residual * residual, axis=-1, keepdims=True)
        direction = residual + (norm_next / (norm_now + small_eps)) * direction
        norm_now = norm_next
    return solution


def reference(user_factors, ratings, block_owner, owner_block_position, block_count):
    lookup = user_factors.reshape(N_USER * UB_DEV, BU, K)
    factor_gram = jnp.dot(user_factors.T, user_factors, preferred_element_type=jnp.float32)
    slot_total = N_USER * NB_CAP
    slot_ids = jnp.arange(slot_total, dtype=jnp.int32)
    identity = jnp.eye(K, dtype=jnp.float32)

    def column(column_index):
        user_block = (block_owner[column_index] * UB_DEV + owner_block_position[column_index]).astype(jnp.int32)
        limits = jnp.repeat(block_count[column_index], NB_CAP)
        active_slots = (slot_ids % NB_CAP) < limits
        begin = (column_index * ITEMS_DEV).astype(jnp.int32)
        weights = lax.dynamic_slice_in_dim(ratings, begin, ITEMS_DEV, 1)
        weights = jnp.where(active_slots[:, None, None], weights, jnp.zeros_like(weights))
        active_status = active_slots.astype(jnp.float32)

        def accumulate(carry, index_in_group):
            gram_part, rhs_part = carry
            leading_slot = (index_in_group * members_per_group).astype(jnp.int32)
            w_group = lax.dynamic_slice_in_dim(weights, leading_slot, members_per_group, 0).astype(jnp.float32)
            picked = lax.dynamic_slice_in_dim(user_block, leading_slot, members_per_group, 0)
            r_group = lookup[picked].astype(jnp.float32)
            local_group_blocks = lax.dynamic_slice_in_dim(active_status, leading_slot, members_per_group, 0)
            rounded = (w_group[:, :, :, None] * r_group[:, None, :, :]).astype(jnp.bfloat16)
            scaled = lax.optimization_barrier(rounded).astype(jnp.float32)
            gram_part = gram_part + jnp.einsum('bjuk,bul->jkl', scaled, r_group, precision=lax.Precision.HIGHEST)
            rhs_part = rhs_part + jnp.einsum('bju,buk->jk', w_group, r_group, precision=lax.Precision.HIGHEST)
            rhs_part = rhs_part + jnp.sum(local_group_blocks[:, None, None] * r_group, axis=(0, 1))[None, :]
            return (gram_part, rhs_part), None

        initial = (jnp.zeros((ITEMS_DEV, K, K), jnp.float32), jnp.zeros((ITEMS_DEV, K), jnp.float32))
        (gram_part, rhs_part), _ = lax.scan(accumulate, initial, jnp.arange(slot_total // members_per_group, dtype=jnp.int32))
        system = gram_part + factor_gram[None, :, :] + ridge_weight * identity[None, :, :]
        return conjugate_solve(system, rhs_part)

    solutions = lax.map(column, jnp.arange(N_ITEM, dtype=jnp.int32))
    return solutions.reshape(ITEMS, K)
```

```python
import jax
import jax.numpy as jnp
from jax import lax
from jax.experimental import pallas as pl
from jax.experimental.pallas import tpu as pltpu
from jax.sharding import PartitionSpec as P

ITERS = 8
MESH = pl.DeviceIdType.MESH


ridge_weight = 0.05
small_eps = 1e-06
group_blocks = 2


def conjugate_solve(system, right_side):
    solution = jnp.zeros_like(right_side)
    residual = right_side
    direction = right_side
    norm_now = jnp.sum(residual * residual, axis=-1, keepdims=True)
    for iteration in range(ITERS):
        image = jnp.einsum("jkl,jl->jk", system, direction, precision=lax.Precision.HIGHEST)
        alpha = norm_now / (jnp.sum(direction * image, axis=-1, keepdims=True) + small_eps)
        solution = solution + alpha * direction
        residual = residual - alpha * image
        norm_next = jnp.sum(residual * residual, axis=-1, keepdims=True)
        direction = residual + norm_next / (norm_now + small_eps) * direction
        norm_now = norm_next
    return solution


def block_terms(weights, block_rows, live_count, item_count):
    block_users = block_rows.shape[1]
    factor_width = block_rows.shape[2]
    group_turns = (live_count + group_blocks - 1) // group_blocks

    def accumulate(index_in_group, carry):
        gram_part, rhs_part = carry
        leading_slot = index_in_group * group_blocks
        w_group = lax.dynamic_slice_in_dim(weights, leading_slot, group_blocks, 0)
        r_group = lax.dynamic_slice_in_dim(block_rows, leading_slot, group_blocks, 0)
        live_mask = (leading_slot + jnp.arange(group_blocks, dtype=jnp.int32) < live_count).astype(
            jnp.bfloat16
        )
        w_group = w_group * live_mask[:, None, None]
        scaled = w_group[:, :, :, None] * r_group[:, None, :, :]
        gram_part = gram_part + jnp.einsum(
            "bjuk,bul->jkl", scaled, r_group, preferred_element_type=jnp.float32
        )
        live_ones = jnp.broadcast_to(live_mask[:, None], (group_blocks, block_users))
        rhs_part = rhs_part + jnp.einsum(
            "bju,buk->jk", w_group, r_group, preferred_element_type=jnp.float32
        )
        rhs_part = (
            rhs_part
            + jnp.einsum("bu,buk->k", live_ones, r_group, preferred_element_type=jnp.float32)[
                None, :
            ]
        )
        return (gram_part, rhs_part)

    initial = (
        jnp.zeros((item_count, factor_width, factor_width), jnp.float32),
        jnp.zeros((item_count, factor_width), jnp.float32),
    )
    gram_part, rhs_part = lax.fori_loop(0, group_turns, accumulate, initial)
    return jnp.concatenate([gram_part, rhs_part[:, None, :]], axis=1)


def on_device(user_factors, ratings, block_owner, owner_block_position, block_count):
    gathered = lax.all_gather(user_factors, "item", axis=0, tiled=True)
    block_users = ratings.shape[2]
    factor_width = gathered.shape[1]
    lookup = gathered.reshape(gathered.shape[0] // block_users, block_users, factor_width)
    owners = block_owner[0]
    local_ids = owner_block_position[0]
    filled = block_count[0, 0]
    peer_count = lax.axis_size("user")
    slot_count = owners.shape[0]
    capacity = max(2, 3 * slot_count // (2 * peer_count))
    onehot = (owners[:, None] == jnp.arange(peer_count, dtype=jnp.int32)[None, :]).astype(jnp.int32)
    before = jnp.cumsum(onehot, axis=0) - onehot
    position = jnp.sum(before * onehot, axis=1)
    requests = jnp.zeros((peer_count, capacity), jnp.int32).at[owners, position].set(local_ids)
    local_gram = jnp.einsum("rk,rl->kl", gathered, gathered, preferred_element_type=jnp.float32)
    fetched = lax.all_to_all(
        lookup[lax.all_to_all(requests, "user", split_axis=0, concat_axis=0, tiled=True)],
        "user",
        split_axis=0,
        concat_axis=0,
        tiled=True,
    )
    block_rows = fetched[owners, position]
    items_here = ratings.shape[1] // peer_count
    summed = lax.psum_scatter(
        block_terms(ratings, block_rows, filled, items_here * lax.axis_size("user")),
        "user",
        scatter_dimension=0,
        tiled=True,
    )
    system = summed[:, :factor_width, :]
    right_side = summed[:, factor_width, :]
    system = system + lax.psum(local_gram, "user")[None, :, :]
    system = system + ridge_weight * jnp.eye(factor_width, dtype=jnp.float32)[None, :, :]
    return conjugate_solve(system, right_side)


def make_kernel(peer_count, item_count, rows_here, capacity, items_dev, weight_rows, factor_width, block_users):
    chip_count = item_count // 2
    half_chips = chip_count // 2
    items_here = items_dev // peer_count
    gram_rows = items_dev * factor_width
    part_rows = factor_width + 8
    tiles_here = rows_here // 16
    block_tiles = block_users // 16

    def kernel(
        factors_ref, weights_ref, meta_ref, out_ref,
        rows, weights_in, meta_in, places, acc, plain, part, part_in,
        chip_send, chip_recv, twin_send, twin_recv,
        weight_send, weight_recv, meta_send, meta_recv, part_send, part_recv, local_sem,
    ):
        me_item = lax.axis_index("item")
        me_user = lax.axis_index("user")
        core = lax.rem(me_item, 2)
        chip = lax.div(me_item, 2)
        chip_x = lax.rem(chip, 2)
        chip_y = lax.div(chip, 2)
        twin = chip * 2 + (1 - core)
        shifts = [(dy, dx) for dy in range(half_chips) for dx in range(2) if dy or dx]

        def chip_at(dy, dx):
            return lax.rem(chip_y + dy, half_chips) * 2 + lax.rem(chip_x + dx, 2)

        def shard(index):
            return rows.at[pl.ds(index * tiles_here, tiles_here)]

        barrier = pltpu.get_barrier_semaphore()
        for dy, dx in shifts:
            pl.semaphore_signal(
                barrier, inc=1, device_id=(chip_at(dy, dx) * 2 + core, me_user), device_id_type=MESH
            )
        pl.semaphore_signal(barrier, inc=1, device_id=(twin, me_user), device_id_type=MESH)
        for d in range(1, peer_count):
            pl.semaphore_signal(
                barrier, inc=1, device_id=(me_item, lax.rem(me_user + d, peer_count)), device_id_type=MESH
            )
        pl.semaphore_wait(barrier, len(shifts) + 1 + peer_count - 1)

        def chip_copy(n, owner, target):
            return pltpu.make_async_remote_copy(
                src_ref=factors_ref, dst_ref=shard(owner),
                send_sem=chip_send.at[n], recv_sem=chip_recv.at[n],
                device_id=(target, me_user), device_id_type=MESH,
            )

        def twin_copy(n, src, owner):
            return pltpu.make_async_remote_copy(
                src_ref=src, dst_ref=shard(owner),
                send_sem=twin_send.at[n], recv_sem=twin_recv.at[n],
                device_id=(twin, me_user), device_id_type=MESH,
            )

        sent = []
        for n, (dy, dx) in enumerate(shifts):
            copy = chip_copy(n, me_item, chip_at(dy, dx) * 2 + core)
            copy.start()
            sent.append(copy)
        copy = twin_copy(0, factors_ref, me_item)
        copy.start()
        sent.append(copy)
        for d in range(1, peer_count):
            target = lax.rem(me_user + d, peer_count)
            copy = pltpu.make_async_remote_copy(
                src_ref=meta_ref.at[target], dst_ref=meta_in.at[d],
                send_sem=meta_send.at[d], recv_sem=meta_recv.at[d],
                device_id=(me_item, target), device_id_type=MESH,
            )
            copy.start()
            sent.append(copy)
            copy = pltpu.make_async_remote_copy(
                src_ref=weights_ref.at[target], dst_ref=weights_in.at[d],
                send_sem=weight_send.at[d], recv_sem=weight_recv.at[d],
                device_id=(me_item, target), device_id_type=MESH,
            )
            copy.start()
            sent.append(copy)
        own_weights = pltpu.make_async_copy(weights_ref.at[me_user], weights_in.at[0], local_sem.at[0])
        own_meta = pltpu.make_async_copy(meta_ref.at[me_user], meta_in.at[0], local_sem.at[1])
        own_rows = pltpu.make_async_copy(factors_ref, shard(me_item), local_sem.at[2])
        own_weights.start()
        own_meta.start()
        own_rows.start()

        def add_plain(block, first=False):
            block = block.reshape(rows_here, factor_width)
            term = lax.dot_general(
                block, block, (((0,), (0,)), ((), ())), preferred_element_type=jnp.float32
            )
            plain[...] = term if first else plain[...] + term

        add_plain(factors_ref[...], True)
        acc[...] = jnp.zeros_like(acc)

        def add_shard(index):
            add_plain(rows[pl.ds(index * tiles_here, tiles_here)])

        for n, (dy, dx) in enumerate(shifts):
            owner = lax.rem(chip_y + half_chips - dy, half_chips) * 2 + lax.rem(chip_x + 2 - dx, 2)
            owner = owner * 2 + core
            chip_copy(n, owner, twin).wait_recv()
            copy = twin_copy(n + 1, shard(owner), owner)
            copy.start()
            sent.append(copy)
            add_shard(owner)
        twin_copy(0, factors_ref, twin).wait_recv()
        add_shard(twin)
        for n, (dy, dx) in enumerate(shifts):
            owner = lax.rem(chip_y + half_chips - dy, half_chips) * 2 + lax.rem(chip_x + 2 - dx, 2)
            owner = owner * 2 + 1 - core
            twin_copy(n + 1, shard(owner), owner).wait_recv()
            add_shard(owner)
        own_weights.wait()
        own_meta.wait()
        own_rows.wait()
        for d in range(1, peer_count):
            pltpu.make_async_remote_copy(
                src_ref=meta_ref.at[0], dst_ref=meta_in.at[d],
                send_sem=meta_send.at[d], recv_sem=meta_recv.at[d],
                device_id=(twin, me_user), device_id_type=MESH,
            ).wait_recv()
            pltpu.make_async_remote_copy(
                src_ref=weights_ref.at[0], dst_ref=weights_in.at[d],
                send_sem=weight_send.at[d], recv_sem=weight_recv.at[d],
                device_id=(twin, me_user), device_id_type=MESH,
            ).wait_recv()
        to_scalar = pltpu.make_async_copy(meta_in, places, local_sem.at[3])
        to_scalar.start()
        to_scalar.wait()

        def slots(i, carry):
            lefts, rights = [], []
            for d in range(peer_count):
                block = rows[pl.ds(places[d, 0, i] * block_tiles, block_tiles)]
                block = block.reshape(block_users, factor_width)
                turned = block.T
                w = weights_in[d, i]
                lefts.append(
                    jnp.concatenate([turned * w[j : j + 1, :] for j in range(items_dev)] + [w], axis=0)
                )
                rights.append(block)
            acc[...] += jnp.dot(
                jnp.concatenate(lefts, axis=1),
                jnp.concatenate(rights, axis=0),
                preferred_element_type=jnp.float32,
            )
            return carry

        lax.fori_loop(0, capacity, slots, 0)

        common = plain[...]
        live_sum = acc[gram_rows + items_dev : gram_rows + items_dev + 1, :]
        for j in range(items_dev):
            owner, place = j // items_here, j % items_here
            part[owner, place, :factor_width, :] = (
                acc[j * factor_width : (j + 1) * factor_width, :] + common
            )
            part[owner, place, factor_width:, :] = jnp.broadcast_to(
                acc[gram_rows + j : gram_rows + j + 1, :] + live_sum, (8, factor_width)
            )
        for d in range(1, peer_count):
            target = lax.rem(me_user + d, peer_count)
            copy = pltpu.make_async_remote_copy(
                src_ref=part.at[target], dst_ref=part_in.at[d - 1],
                send_sem=part_send.at[d], recv_sem=part_recv.at[d],
                device_id=(me_item, target), device_id_type=MESH,
            )
            copy.start()
            sent.append(copy)
        for d in range(1, peer_count):
            pltpu.make_async_remote_copy(
                src_ref=part.at[0], dst_ref=part_in.at[d - 1],
                send_sem=part_send.at[d], recv_sem=part_recv.at[d],
                device_id=(twin, me_user), device_id_type=MESH,
            ).wait_recv()

        row_at = lax.broadcasted_iota(jnp.int32, (factor_width, factor_width), 0)
        col_at = lax.broadcasted_iota(jnp.int32, (factor_width, factor_width), 1)
        diagonal = row_at == col_at
        for place in range(items_here):
            whole = part[me_user, place]
            for d in range(1, peer_count):
                whole = whole + part_in[d - 1, place]
            system = whole[:factor_width] + jnp.where(diagonal, ridge_weight, 0.0)
            residual = whole[factor_width : factor_width + 1]
            answer = jnp.zeros_like(residual)
            direction = residual
            norm_now = jnp.sum(residual * residual, axis=1, keepdims=True)
            for _ in range(ITERS):
                image = jnp.sum(system * direction, axis=1, keepdims=True)
                image = jnp.sum(jnp.where(diagonal, image, 0.0), axis=0, keepdims=True)
                alpha = norm_now / (jnp.sum(direction * image, axis=1, keepdims=True) + small_eps)
                answer = answer + alpha * direction
                residual = residual - alpha * image
                norm_next = jnp.sum(residual * residual, axis=1, keepdims=True)
                direction = residual + norm_next / (norm_now + small_eps) * direction
                norm_now = norm_next
            out_ref[place : place + 1, :] = answer
        for copy in sent:
            copy.wait_send()

    vmem = pl.BlockSpec(memory_space=pltpu.VMEM)
    dma = pltpu.SemaphoreType.DMA
    return pl.pallas_call(
        kernel,
        out_shape=jax.ShapeDtypeStruct((items_here, factor_width), jnp.float32),
        in_specs=[vmem] * 3,
        out_specs=vmem,
        scratch_shapes=[
            pltpu.VMEM((item_count * tiles_here, 16, factor_width), jnp.bfloat16),
            pltpu.VMEM((peer_count, capacity, weight_rows, block_users), jnp.bfloat16),
            pltpu.VMEM((peer_count, 8, 128), jnp.int32),
            pltpu.SMEM((peer_count, 8, 128), jnp.int32),
            pltpu.VMEM((gram_rows + weight_rows, factor_width), jnp.float32),
            pltpu.VMEM((factor_width, factor_width), jnp.float32),
            pltpu.VMEM((peer_count, items_here, part_rows, factor_width), jnp.float32),
            pltpu.VMEM((peer_count - 1, items_here, part_rows, factor_width), jnp.float32),
            dma((chip_count,)), dma((chip_count,)), dma((chip_count,)), dma((chip_count,)),
            dma((peer_count,)), dma((peer_count,)), dma((peer_count,)), dma((peer_count,)),
            dma((peer_count,)), dma((peer_count,)), dma((4,)),
        ],
        compiler_params=pltpu.CompilerParams(
            collective_id=0, has_side_effects=True, vmem_limit_bytes=32 * 1024 * 1024
        ),
    )


def sends_ratings(user_factors, ratings, block_owner, owner_block_position, block_count):
    rows_here, factor_width = user_factors.shape
    slot_count, items_dev, block_users = ratings.shape
    peer_count = lax.axis_size("user")
    item_count = lax.axis_size("item")
    capacity = max(2, 3 * slot_count // (2 * peer_count))
    weight_rows = (items_dev + 1 + 15) // 16 * 16
    owners = block_owner[0]
    local_ids = owner_block_position[0]
    slot_at = jnp.arange(slot_count, dtype=jnp.int32)
    earlier = (owners[None, :] == owners[:, None]) & (slot_at[None, :] < slot_at[:, None])
    code = owners * capacity + jnp.sum(earlier.astype(jnp.int32), axis=1)
    code = jnp.where(slot_at < block_count[0, 0], code, -1)
    chosen = jnp.arange(peer_count * capacity, dtype=jnp.int32)[:, None] == code[None, :]
    places = jnp.sum(jnp.where(chosen, local_ids[None, :], 0), axis=1).reshape(peer_count, 1, capacity)
    meta = jnp.pad(places, ((0, 0), (0, 7), (0, 128 - capacity)))
    padded = jnp.concatenate(
        [
            ratings,
            jnp.ones((slot_count, 1, block_users), jnp.bfloat16),
            jnp.zeros((slot_count, weight_rows - items_dev - 1, block_users), jnp.bfloat16),
        ],
        axis=1,
    )
    weights = jnp.einsum("rs,sju->rju", chosen.astype(jnp.bfloat16), padded)
    weights = weights.reshape(peer_count, capacity, weight_rows, block_users)
    kernel = make_kernel(
        peer_count, item_count, rows_here, capacity, items_dev, weight_rows, factor_width, block_users
    )
    return kernel(user_factors.reshape(rows_here // 16, 16, factor_width), weights, meta)


def by_shape(user_factors, ratings, block_owner, owner_block_position, block_count):
    body = sends_ratings if user_factors.shape[0] % 16 == 0 else on_device
    return body(user_factors, ratings, block_owner, owner_block_position, block_count)


def solution(mesh):
    in_specs = (
        P(("user", "item"), None),
        P("user", "item", None),
        P("item", "user"),
        P("item", "user"),
        P("item", "user"),
    )
    out_specs = P(("item", "user"), None)
    return jax.shard_map(
        by_shape, mesh=mesh, in_specs=in_specs, out_specs=out_specs, check_vma=False
    )
```

```python
import jax
import jax.numpy as jnp
from jax import lax
from jax.experimental import pallas as pl
from jax.experimental.pallas import tpu as pltpu
from jax.sharding import PartitionSpec as P

ITERS = 8
MESH = pl.DeviceIdType.MESH


ridge_weight = 0.05
small_eps = 1e-06
group_blocks = 2


def conjugate_solve(system, right_side):
    solution = jnp.zeros_like(right_side)
    residual = right_side
    direction = right_side
    norm_now = jnp.sum(residual * residual, axis=-1, keepdims=True)
    for iteration in range(ITERS):
        image = jnp.einsum("jkl,jl->jk", system, direction, precision=lax.Precision.HIGHEST)
        alpha = norm_now / (jnp.sum(direction * image, axis=-1, keepdims=True) + small_eps)
        solution = solution + alpha * direction
        residual = residual - alpha * image
        norm_next = jnp.sum(residual * residual, axis=-1, keepdims=True)
        direction = residual + norm_next / (norm_now + small_eps) * direction
        norm_now = norm_next
    return solution


def block_terms(weights, block_rows, live_count, item_count):
    block_users = block_rows.shape[1]
    factor_width = block_rows.shape[2]
    group_turns = (live_count + group_blocks - 1) // group_blocks

    def accumulate(index_in_group, carry):
        gram_part, rhs_part = carry
        leading_slot = index_in_group * group_blocks
        w_group = lax.dynamic_slice_in_dim(weights, leading_slot, group_blocks, 0)
        r_group = lax.dynamic_slice_in_dim(block_rows, leading_slot, group_blocks, 0)
        live_mask = (leading_slot + jnp.arange(group_blocks, dtype=jnp.int32) < live_count).astype(
            jnp.bfloat16
        )
        w_group = w_group * live_mask[:, None, None]
        scaled = w_group[:, :, :, None] * r_group[:, None, :, :]
        gram_part = gram_part + jnp.einsum(
            "bjuk,bul->jkl", scaled, r_group, preferred_element_type=jnp.float32
        )
        live_ones = jnp.broadcast_to(live_mask[:, None], (group_blocks, block_users))
        rhs_part = rhs_part + jnp.einsum(
            "bju,buk->jk", w_group, r_group, preferred_element_type=jnp.float32
        )
        rhs_part = (
            rhs_part
            + jnp.einsum("bu,buk->k", live_ones, r_group, preferred_element_type=jnp.float32)[
                None, :
            ]
        )
        return (gram_part, rhs_part)

    initial = (
        jnp.zeros((item_count, factor_width, factor_width), jnp.float32),
        jnp.zeros((item_count, factor_width), jnp.float32),
    )
    gram_part, rhs_part = lax.fori_loop(0, group_turns, accumulate, initial)
    return jnp.concatenate([gram_part, rhs_part[:, None, :]], axis=1)


def on_device(user_factors, ratings, block_owner, owner_block_position, block_count):
    gathered = lax.all_gather(user_factors, "item", axis=0, tiled=True)
    block_users = ratings.shape[2]
    factor_width = gathered.shape[1]
    lookup = gathered.reshape(gathered.shape[0] // block_users, block_users, factor_width)
    owners = block_owner[0]
    local_ids = owner_block_position[0]
    filled = block_count[0, 0]
    peer_count = lax.axis_size("user")
    slot_count = owners.shape[0]
    capacity = max(2, 3 * slot_count // (2 * peer_count))
    onehot = (owners[:, None] == jnp.arange(peer_count, dtype=jnp.int32)[None, :]).astype(jnp.int32)
    before = jnp.cumsum(onehot, axis=0) - onehot
    position = jnp.sum(before * onehot, axis=1)
    requests = jnp.zeros((peer_count, capacity), jnp.int32).at[owners, position].set(local_ids)
    local_gram = jnp.einsum("rk,rl->kl", gathered, gathered, preferred_element_type=jnp.float32)
    fetched = lax.all_to_all(
        lookup[lax.all_to_all(requests, "user", split_axis=0, concat_axis=0, tiled=True)],
        "user",
        split_axis=0,
        concat_axis=0,
        tiled=True,
    )
    block_rows = fetched[owners, position]
    items_here = ratings.shape[1] // peer_count
    summed = lax.psum_scatter(
        block_terms(ratings, block_rows, filled, items_here * lax.axis_size("user")),
        "user",
        scatter_dimension=0,
        tiled=True,
    )
    system = summed[:, :factor_width, :]
    right_side = summed[:, factor_width, :]
    system = system + lax.psum(local_gram, "user")[None, :, :]
    system = system + ridge_weight * jnp.eye(factor_width, dtype=jnp.float32)[None, :, :]
    return conjugate_solve(system, right_side)


def make_kernel(peer_count, item_count, rows_here, capacity, items_dev, weight_rows, factor_width, block_users):
    chip_count = item_count // 2
    half_chips = chip_count // 2
    items_here = items_dev // peer_count
    gram_rows = items_dev * factor_width
    part_rows = factor_width + 8
    tiles_here = rows_here // 16
    block_tiles = block_users // 16

    def kernel(
        factors_ref, weights_ref, meta_ref, out_ref,
        rows, weights_in, meta_in, places, acc, plain, part, part_in,
        chip_send, chip_recv, twin_send, twin_recv,
        weight_send, weight_recv, meta_send, meta_recv, part_send, part_recv, local_sem,
    ):
        me_item = lax.axis_index("item")
        me_user = lax.axis_index("user")
        core = lax.rem(me_item, 2)
        chip = lax.div(me_item, 2)
        chip_x = lax.rem(chip, 2)
        chip_y = lax.div(chip, 2)
        twin = chip * 2 + (1 - core)
        shifts = [(dy, dx) for dy in range(half_chips) for dx in range(2) if dy or dx]

        def chip_at(dy, dx):
            return lax.rem(chip_y + dy, half_chips) * 2 + lax.rem(chip_x + dx, 2)

        across, along, corner = chip_at(0, 1), chip_at(1, 0), chip_at(1, 1)
        first = tiles_here // 2
        moves = [
            (across, 0, across), (along, 1, along), (across, 1, across),
            (along, 0, along), (corner, 0, along), (corner, 1, across),
        ]

        def shard(index):
            return rows.at[pl.ds(index * tiles_here, tiles_here)]

        def half_of(ref, start, half):
            return ref.at[pl.ds(start + half * first, tiles_here - first if half else first)]

        def half_shard(index, half):
            return half_of(rows, index * tiles_here, half)

        barrier = pltpu.get_barrier_semaphore()
        for dy, dx in shifts:
            pl.semaphore_signal(
                barrier, inc=1, device_id=(chip_at(dy, dx) * 2 + core, me_user), device_id_type=MESH
            )
        pl.semaphore_signal(barrier, inc=1, device_id=(twin, me_user), device_id_type=MESH)
        for d in range(1, peer_count):
            pl.semaphore_signal(
                barrier, inc=1, device_id=(me_item, lax.rem(me_user + d, peer_count)), device_id_type=MESH
            )
        pl.semaphore_wait(barrier, len(shifts) + 1 + peer_count - 1)

        def chip_copy(n, src, owner):
            return pltpu.make_async_remote_copy(
                src_ref=src, dst_ref=half_shard(owner, moves[n][1]),
                send_sem=chip_send.at[n], recv_sem=chip_recv.at[n],
                device_id=(moves[n][2] * 2 + core, me_user), device_id_type=MESH,
            )

        def twin_copy(n, src, dst):
            return pltpu.make_async_remote_copy(
                src_ref=src, dst_ref=dst,
                send_sem=twin_send.at[n], recv_sem=twin_recv.at[n],
                device_id=(twin, me_user), device_id_type=MESH,
            )

        sent = []
        for n in range(4):
            copy = chip_copy(n, half_of(factors_ref, 0, moves[n][1]), me_item)
            copy.start()
            sent.append(copy)
        copy = twin_copy(6, factors_ref, shard(me_item))
        copy.start()
        sent.append(copy)
        for d in range(1, peer_count):
            target = lax.rem(me_user + d, peer_count)
            copy = pltpu.make_async_remote_copy(
                src_ref=meta_ref.at[target], dst_ref=meta_in.at[d],
                send_sem=meta_send.at[d], recv_sem=meta_recv.at[d],
                device_id=(me_item, target), device_id_type=MESH,
            )
            copy.start()
            sent.append(copy)
            copy = pltpu.make_async_remote_copy(
                src_ref=weights_ref.at[target], dst_ref=weights_in.at[d],
                send_sem=weight_send.at[d], recv_sem=weight_recv.at[d],
                device_id=(me_item, target), device_id_type=MESH,
            )
            copy.start()
            sent.append(copy)
        own_weights = pltpu.make_async_copy(weights_ref.at[me_user], weights_in.at[0], local_sem.at[0])
        own_meta = pltpu.make_async_copy(meta_ref.at[me_user], meta_in.at[0], local_sem.at[1])
        own_rows = pltpu.make_async_copy(factors_ref, shard(me_item), local_sem.at[2])
        own_weights.start()
        own_meta.start()
        own_rows.start()

        def add_plain(block, opening=False):
            block = block.reshape(rows_here, factor_width)
            term = lax.dot_general(
                block, block, (((0,), (0,)), ((), ())), preferred_element_type=jnp.float32
            )
            plain[...] = term if opening else plain[...] + term

        add_plain(factors_ref[...], True)
        acc[...] = jnp.zeros_like(acc)

        def add_shard(index):
            add_plain(rows[pl.ds(index * tiles_here, tiles_here)])

        def arrived(n):
            piece = half_shard(moves[n][0] * 2 + core, moves[n][1])
            chip_copy(n, piece, moves[n][0] * 2 + core).wait_recv()
            if n < 2:
                onward = chip_copy(n + 4, piece, moves[n][0] * 2 + core)
                onward.start()
                sent.append(onward)
            handed = twin_copy(n, piece, piece)
            handed.start()
            sent.append(handed)

        def twin_arrived(n):
            piece = half_shard(moves[n][0] * 2 + 1 - core, moves[n][1])
            twin_copy(n, piece, piece).wait_recv()

        arrived(0)
        arrived(1)
        twin_copy(6, factors_ref, shard(twin)).wait_recv()
        add_shard(twin)
        arrived(2)
        arrived(3)
        add_shard(across * 2 + core)
        add_shard(along * 2 + core)
        for n in range(4):
            twin_arrived(n)
        add_shard(across * 2 + 1 - core)
        add_shard(along * 2 + 1 - core)
        arrived(4)
        arrived(5)
        add_shard(corner * 2 + core)
        twin_arrived(4)
        twin_arrived(5)
        add_shard(corner * 2 + 1 - core)
        own_weights.wait()
        own_meta.wait()
        own_rows.wait()
        for d in range(1, peer_count):
            pltpu.make_async_remote_copy(
                src_ref=meta_ref.at[0], dst_ref=meta_in.at[d],
                send_sem=meta_send.at[d], recv_sem=meta_recv.at[d],
                device_id=(twin, me_user), device_id_type=MESH,
            ).wait_recv()
            pltpu.make_async_remote_copy(
                src_ref=weights_ref.at[0], dst_ref=weights_in.at[d],
                send_sem=weight_send.at[d], recv_sem=weight_recv.at[d],
                device_id=(twin, me_user), device_id_type=MESH,
            ).wait_recv()
        to_scalar = pltpu.make_async_copy(meta_in, places, local_sem.at[3])
        to_scalar.start()
        to_scalar.wait()

        def slots(i, carry):
            lefts, rights = [], []
            for d in range(peer_count):
                block = rows[pl.ds(places[d, 0, i] * block_tiles, block_tiles)]
                block = block.reshape(block_users, factor_width)
                turned = block.T
                w = weights_in[d, i]
                lefts.append(
                    jnp.concatenate([turned * w[j : j + 1, :] for j in range(items_dev)] + [w], axis=0)
                )
                rights.append(block)
            acc[...] += jnp.dot(
                jnp.concatenate(lefts, axis=1),
                jnp.concatenate(rights, axis=0),
                preferred_element_type=jnp.float32,
            )
            return carry

        lax.fori_loop(0, capacity, slots, 0, unroll=7)

        common = plain[...]
        live_sum = acc[gram_rows + items_dev : gram_rows + items_dev + 1, :]
        for j in range(items_dev):
            owner, place = j // items_here, j % items_here
            part[owner, place, :factor_width, :] = (
                acc[j * factor_width : (j + 1) * factor_width, :] + common
            )
            part[owner, place, factor_width:, :] = jnp.broadcast_to(
                acc[gram_rows + j : gram_rows + j + 1, :] + live_sum, (8, factor_width)
            )
        for d in range(1, peer_count):
            target = lax.rem(me_user + d, peer_count)
            copy = pltpu.make_async_remote_copy(
                src_ref=part.at[target], dst_ref=part_in.at[d - 1],
                send_sem=part_send.at[d], recv_sem=part_recv.at[d],
                device_id=(me_item, target), device_id_type=MESH,
            )
            copy.start()
            sent.append(copy)
        for d in range(1, peer_count):
            pltpu.make_async_remote_copy(
                src_ref=part.at[0], dst_ref=part_in.at[d - 1],
                send_sem=part_send.at[d], recv_sem=part_recv.at[d],
                device_id=(twin, me_user), device_id_type=MESH,
            ).wait_recv()

        row_at = lax.broadcasted_iota(jnp.int32, (factor_width, factor_width), 0)
        col_at = lax.broadcasted_iota(jnp.int32, (factor_width, factor_width), 1)
        diagonal = row_at == col_at
        for place in range(items_here):
            whole = part[me_user, place]
            for d in range(1, peer_count):
                whole = whole + part_in[d - 1, place]
            system = whole[:factor_width] + jnp.where(diagonal, ridge_weight, 0.0)
            residual = whole[factor_width : factor_width + 1]
            answer = jnp.zeros_like(residual)
            direction = residual
            norm_now = jnp.sum(residual * residual, axis=1, keepdims=True)
            for _ in range(ITERS):
                image = jnp.sum(system * direction, axis=1, keepdims=True)
                image = jnp.sum(jnp.where(diagonal, image, 0.0), axis=0, keepdims=True)
                alpha = norm_now / (jnp.sum(direction * image, axis=1, keepdims=True) + small_eps)
                answer = answer + alpha * direction
                residual = residual - alpha * image
                norm_next = jnp.sum(residual * residual, axis=1, keepdims=True)
                direction = residual + norm_next / (norm_now + small_eps) * direction
                norm_now = norm_next
            out_ref[place : place + 1, :] = answer
        for copy in sent:
            copy.wait_send()

    vmem = pl.BlockSpec(memory_space=pltpu.VMEM)
    dma = pltpu.SemaphoreType.DMA
    return pl.pallas_call(
        kernel,
        out_shape=jax.ShapeDtypeStruct((items_here, factor_width), jnp.float32),
        in_specs=[vmem] * 3,
        out_specs=vmem,
        scratch_shapes=[
            pltpu.VMEM((item_count * tiles_here, 16, factor_width), jnp.bfloat16),
            pltpu.VMEM((peer_count, capacity, weight_rows, block_users), jnp.bfloat16),
            pltpu.VMEM((peer_count, 8, 128), jnp.int32),
            pltpu.SMEM((peer_count, 8, 128), jnp.int32),
            pltpu.VMEM((gram_rows + weight_rows, factor_width), jnp.float32),
            pltpu.VMEM((factor_width, factor_width), jnp.float32),
            pltpu.VMEM((peer_count, items_here, part_rows, factor_width), jnp.float32),
            pltpu.VMEM((peer_count - 1, items_here, part_rows, factor_width), jnp.float32),
            dma((6,)), dma((6,)), dma((7,)), dma((7,)),
            dma((peer_count,)), dma((peer_count,)), dma((peer_count,)), dma((peer_count,)),
            dma((peer_count,)), dma((peer_count,)), dma((4,)),
        ],
        compiler_params=pltpu.CompilerParams(
            collective_id=0, has_side_effects=True, vmem_limit_bytes=32 * 1024 * 1024
        ),
    )


def sends_ratings(user_factors, ratings, block_owner, owner_block_position, block_count):
    rows_here, factor_width = user_factors.shape
    slot_count, items_dev, block_users = ratings.shape
    peer_count = lax.axis_size("user")
    item_count = lax.axis_size("item")
    capacity = max(2, 3 * slot_count // (2 * peer_count))
    weight_rows = (items_dev + 1 + 15) // 16 * 16
    owners = block_owner[0]
    local_ids = owner_block_position[0]
    slot_at = jnp.arange(slot_count, dtype=jnp.int32)
    earlier = (owners[None, :] == owners[:, None]) & (slot_at[None, :] < slot_at[:, None])
    code = owners * capacity + jnp.sum(earlier.astype(jnp.int32), axis=1)
    code = jnp.where(slot_at < block_count[0, 0], code, -1)
    chosen = jnp.arange(peer_count * capacity, dtype=jnp.int32)[:, None] == code[None, :]
    places = jnp.sum(jnp.where(chosen, local_ids[None, :], 0), axis=1).reshape(peer_count, 1, capacity)
    meta = jnp.pad(places, ((0, 0), (0, 7), (0, 128 - capacity)))
    padded = jnp.concatenate(
        [
            ratings,
            jnp.ones((slot_count, 1, block_users), jnp.bfloat16),
            jnp.zeros((slot_count, weight_rows - items_dev - 1, block_users), jnp.bfloat16),
        ],
        axis=1,
    )
    weights = jnp.einsum("rs,sju->rju", chosen.astype(jnp.bfloat16), padded)
    weights = weights.reshape(peer_count, capacity, weight_rows, block_users)
    kernel = make_kernel(
        peer_count, item_count, rows_here, capacity, items_dev, weight_rows, factor_width, block_users
    )
    return kernel(user_factors.reshape(rows_here // 16, 16, factor_width), weights, meta)


def by_shape(user_factors, ratings, block_owner, owner_block_position, block_count):
    fits = user_factors.shape[0] % 16 == 0 and lax.axis_size("item") == 8
    body = sends_ratings if fits else on_device
    return body(user_factors, ratings, block_owner, owner_block_position, block_count)


def solution(mesh):
    in_specs = (
        P(("user", "item"), None),
        P("user", "item", None),
        P("item", "user"),
        P("item", "user"),
        P("item", "user"),
    )
    out_specs = P(("item", "user"), None)
    return jax.shard_map(
        by_shape, mesh=mesh, in_specs=in_specs, out_specs=out_specs, check_vma=False
    )
```

```python
import jax
import jax.numpy as jnp
from jax import lax
from jax.experimental import pallas as pl
from jax.experimental.pallas import tpu as pltpu
from jax.sharding import PartitionSpec as P

ITERS = 8
MESH = pl.DeviceIdType.MESH


ridge_weight = 0.05
small_eps = 1e-06
group_blocks = 2


def conjugate_solve(system, right_side):
    solution = jnp.zeros_like(right_side)
    residual = right_side
    direction = right_side
    norm_now = jnp.sum(residual * residual, axis=-1, keepdims=True)
    for iteration in range(ITERS):
        image = jnp.einsum("jkl,jl->jk", system, direction, precision=lax.Precision.HIGHEST)
        alpha = norm_now / (jnp.sum(direction * image, axis=-1, keepdims=True) + small_eps)
        solution = solution + alpha * direction
        residual = residual - alpha * image
        norm_next = jnp.sum(residual * residual, axis=-1, keepdims=True)
        direction = residual + norm_next / (norm_now + small_eps) * direction
        norm_now = norm_next
    return solution


def block_terms(weights, block_rows, live_count, item_count):
    block_users = block_rows.shape[1]
    factor_width = block_rows.shape[2]
    group_turns = (live_count + group_blocks - 1) // group_blocks

    def accumulate(index_in_group, carry):
        gram_part, rhs_part = carry
        leading_slot = index_in_group * group_blocks
        w_group = lax.dynamic_slice_in_dim(weights, leading_slot, group_blocks, 0)
        r_group = lax.dynamic_slice_in_dim(block_rows, leading_slot, group_blocks, 0)
        live_mask = (leading_slot + jnp.arange(group_blocks, dtype=jnp.int32) < live_count).astype(
            jnp.bfloat16
        )
        w_group = w_group * live_mask[:, None, None]
        scaled = w_group[:, :, :, None] * r_group[:, None, :, :]
        gram_part = gram_part + jnp.einsum(
            "bjuk,bul->jkl", scaled, r_group, preferred_element_type=jnp.float32
        )
        live_ones = jnp.broadcast_to(live_mask[:, None], (group_blocks, block_users))
        rhs_part = rhs_part + jnp.einsum(
            "bju,buk->jk", w_group, r_group, preferred_element_type=jnp.float32
        )
        rhs_part = (
            rhs_part
            + jnp.einsum("bu,buk->k", live_ones, r_group, preferred_element_type=jnp.float32)[
                None, :
            ]
        )
        return (gram_part, rhs_part)

    initial = (
        jnp.zeros((item_count, factor_width, factor_width), jnp.float32),
        jnp.zeros((item_count, factor_width), jnp.float32),
    )
    gram_part, rhs_part = lax.fori_loop(0, group_turns, accumulate, initial)
    return jnp.concatenate([gram_part, rhs_part[:, None, :]], axis=1)


def on_device(user_factors, ratings, block_owner, owner_block_position, block_count):
    gathered = lax.all_gather(user_factors, "item", axis=0, tiled=True)
    block_users = ratings.shape[2]
    factor_width = gathered.shape[1]
    lookup = gathered.reshape(gathered.shape[0] // block_users, block_users, factor_width)
    owners = block_owner[0]
    local_ids = owner_block_position[0]
    filled = block_count[0, 0]
    peer_count = lax.axis_size("user")
    slot_count = owners.shape[0]
    capacity = max(2, 3 * slot_count // (2 * peer_count))
    onehot = (owners[:, None] == jnp.arange(peer_count, dtype=jnp.int32)[None, :]).astype(jnp.int32)
    before = jnp.cumsum(onehot, axis=0) - onehot
    position = jnp.sum(before * onehot, axis=1)
    requests = jnp.zeros((peer_count, capacity), jnp.int32).at[owners, position].set(local_ids)
    local_gram = jnp.einsum("rk,rl->kl", gathered, gathered, preferred_element_type=jnp.float32)
    fetched = lax.all_to_all(
        lookup[lax.all_to_all(requests, "user", split_axis=0, concat_axis=0, tiled=True)],
        "user",
        split_axis=0,
        concat_axis=0,
        tiled=True,
    )
    block_rows = fetched[owners, position]
    items_here = ratings.shape[1] // peer_count
    summed = lax.psum_scatter(
        block_terms(ratings, block_rows, filled, items_here * lax.axis_size("user")),
        "user",
        scatter_dimension=0,
        tiled=True,
    )
    system = summed[:, :factor_width, :]
    right_side = summed[:, factor_width, :]
    system = system + lax.psum(local_gram, "user")[None, :, :]
    system = system + ridge_weight * jnp.eye(factor_width, dtype=jnp.float32)[None, :, :]
    return conjugate_solve(system, right_side)


def make_kernel(peer_count, item_count, rows_here, slot_count, capacity, items_dev, factor_width, block_users):
    chip_count = item_count // 2
    half_chips = chip_count // 2
    items_here = items_dev // peer_count
    gram_rows = items_dev * factor_width
    part_rows = factor_width + 8
    weight_rows = (items_dev + 1 + 15) // 16 * 16
    held = (capacity + 15) // 16 * 16
    lanes = peer_count * held
    tiles_here = rows_here // 16
    block_tiles = block_users // 16

    def kernel(
        factors_ref, ratings_ref, owners_ref, ids_ref, count_ref, out_ref,
        rows, weights_out, weights_in, weights, meta_out, meta_in, places, acc, plain, part, part_in,
        chip_send, chip_recv, twin_send, twin_recv,
        weight_send, weight_recv, meta_send, meta_recv, part_send, part_recv, local_sem,
    ):
        me_item = lax.axis_index("item")
        me_user = lax.axis_index("user")
        core = lax.rem(me_item, 2)
        chip = lax.div(me_item, 2)
        chip_x = lax.rem(chip, 2)
        chip_y = lax.div(chip, 2)
        twin = chip * 2 + (1 - core)
        shifts = [(dy, dx) for dy in range(half_chips) for dx in range(2) if dy or dx]

        def chip_at(dy, dx):
            return lax.rem(chip_y + dy, half_chips) * 2 + lax.rem(chip_x + dx, 2)

        across, along, corner = chip_at(0, 1), chip_at(1, 0), chip_at(1, 1)
        first = tiles_here // 2
        moves = [
            (across, 0, across), (along, 1, along), (across, 1, across),
            (along, 0, along), (corner, 0, along), (corner, 1, across),
        ]

        def shard(index):
            return rows.at[pl.ds(index * tiles_here, tiles_here)]

        def half_of(ref, start, half):
            return ref.at[pl.ds(start + half * first, tiles_here - first if half else first)]

        def half_shard(index, half):
            return half_of(rows, index * tiles_here, half)

        barrier = pltpu.get_barrier_semaphore()
        for dy, dx in shifts:
            pl.semaphore_signal(
                barrier, inc=1, device_id=(chip_at(dy, dx) * 2 + core, me_user), device_id_type=MESH
            )
        pl.semaphore_signal(barrier, inc=1, device_id=(twin, me_user), device_id_type=MESH)
        for d in range(1, peer_count):
            pl.semaphore_signal(
                barrier, inc=1, device_id=(me_item, lax.rem(me_user + d, peer_count)), device_id_type=MESH
            )
        pl.semaphore_wait(barrier, len(shifts) + 1 + peer_count - 1)

        def chip_copy(n, src, owner):
            return pltpu.make_async_remote_copy(
                src_ref=src, dst_ref=half_shard(owner, moves[n][1]),
                send_sem=chip_send.at[n], recv_sem=chip_recv.at[n],
                device_id=(moves[n][2] * 2 + core, me_user), device_id_type=MESH,
            )

        def twin_copy(n, src, dst):
            return pltpu.make_async_remote_copy(
                src_ref=src, dst_ref=dst,
                send_sem=twin_send.at[n], recv_sem=twin_recv.at[n],
                device_id=(twin, me_user), device_id_type=MESH,
            )

        sent = []
        for n in range(4):
            copy = chip_copy(n, half_of(factors_ref, 0, moves[n][1]), me_item)
            copy.start()
            sent.append(copy)
        copy = twin_copy(6, factors_ref, shard(me_item))
        copy.start()
        sent.append(copy)
        own_rows = pltpu.make_async_copy(factors_ref, shard(me_item), local_sem.at[0])
        own_rows.start()

        owners = jnp.broadcast_to(owners_ref[...], (slot_count, slot_count))
        from_slot = lax.broadcasted_iota(jnp.int32, (slot_count, slot_count), 0)
        to_slot = lax.broadcasted_iota(jnp.int32, (slot_count, slot_count), 1)
        owners_down = jnp.sum(jnp.where(from_slot == to_slot, owners, 0), axis=1, keepdims=True)
        earlier = (owners_down == owners) & (from_slot < to_slot)
        rank = jnp.sum(jnp.where(earlier, 1, 0), axis=0, keepdims=True)
        code = jnp.where(to_slot[:1] < count_ref[0, 0], owners[:1] * held + rank, -1)
        chosen = lax.broadcasted_iota(jnp.int32, (lanes, slot_count), 0) == code
        ids = jnp.broadcast_to(ids_ref[...], (lanes, slot_count))
        ids_down = jnp.sum(jnp.where(chosen, ids, 0), axis=1, keepdims=True)
        place_row = lax.broadcasted_iota(jnp.int32, (lanes, lanes), 0)
        place_col = lax.broadcasted_iota(jnp.int32, (lanes, lanes), 1)
        ids_across = jnp.sum(jnp.where(place_row == place_col, ids_down, 0), axis=0, keepdims=True)
        meta_out[...] = jnp.broadcast_to(ids_across, (8, lanes))
        meta_in[0] = meta_out[...]
        picker = jnp.where(chosen, 1.0, 0.0).astype(jnp.bfloat16)
        for j in range(items_dev + 1):
            if j < items_dev:
                plane = ratings_ref[:, j, :]
            else:
                plane = jnp.ones((slot_count, block_users), jnp.bfloat16)
            picked = jnp.dot(picker, plane, preferred_element_type=jnp.float32).astype(jnp.bfloat16)
            for d in range(peer_count):
                weights_out[d, j] = picked[d * held : (d + 1) * held]

        def meta_copy(d, target):
            return pltpu.make_async_remote_copy(
                src_ref=meta_out, dst_ref=meta_in.at[d],
                send_sem=meta_send.at[d], recv_sem=meta_recv.at[d],
                device_id=(me_item, target), device_id_type=MESH,
            )

        def weight_copy(d, target):
            return pltpu.make_async_remote_copy(
                src_ref=weights_out.at[target], dst_ref=weights_in.at[d - 1],
                send_sem=weight_send.at[d], recv_sem=weight_recv.at[d],
                device_id=(me_item, target), device_id_type=MESH,
            )

        for d in range(1, peer_count):
            target = lax.rem(me_user + d, peer_count)
            for copy in (meta_copy(d, target), weight_copy(d, target)):
                copy.start()
                sent.append(copy)

        def add_plain(block, opening=False):
            block = block.reshape(rows_here, factor_width)
            term = lax.dot_general(
                block, block, (((0,), (0,)), ((), ())), preferred_element_type=jnp.float32
            )
            plain[...] = term if opening else plain[...] + term

        add_plain(factors_ref[...], True)
        acc[...] = jnp.zeros_like(acc)

        def add_shard(index):
            add_plain(rows[pl.ds(index * tiles_here, tiles_here)])

        def arrived(n):
            piece = half_shard(moves[n][0] * 2 + core, moves[n][1])
            chip_copy(n, piece, moves[n][0] * 2 + core).wait_recv()
            if n < 2:
                onward = chip_copy(n + 4, piece, moves[n][0] * 2 + core)
                onward.start()
                sent.append(onward)
            handed = twin_copy(n, piece, piece)
            handed.start()
            sent.append(handed)

        def twin_arrived(n):
            piece = half_shard(moves[n][0] * 2 + 1 - core, moves[n][1])
            twin_copy(n, piece, piece).wait_recv()

        arrived(0)
        arrived(1)
        twin_copy(6, factors_ref, shard(twin)).wait_recv()
        add_shard(twin)
        arrived(2)
        arrived(3)
        add_shard(across * 2 + core)
        add_shard(along * 2 + core)
        for d in range(1, peer_count):
            meta_copy(d, lax.rem(me_user + d, peer_count)).wait_recv()
        to_scalar = pltpu.make_async_copy(meta_in, places, local_sem.at[1])
        to_scalar.start()
        weights[0] = weights_out[me_user].astype(jnp.float32)
        for d in range(1, peer_count):
            weight_copy(d, lax.rem(me_user + d, peer_count)).wait_recv()
            weights[d] = weights_in[d - 1].astype(jnp.float32)
        arrived(4)
        arrived(5)
        for n in range(4):
            twin_arrived(n)
        add_shard(across * 2 + 1 - core)
        add_shard(along * 2 + 1 - core)
        add_shard(corner * 2 + core)
        own_rows.wait()
        to_scalar.wait()
        twin_arrived(4)
        twin_arrived(5)
        add_shard(corner * 2 + 1 - core)

        extra_row = lax.broadcasted_iota(jnp.int32, (weight_rows, block_users), 0)

        def slots(i, carry):
            lefts, rights = [], []
            for d in range(peer_count):
                block = rows[pl.ds(places[d, 0, me_user * held + i] * block_tiles, block_tiles)]
                block = block.reshape(block_users, factor_width)
                turned = block.T
                left = []
                extra = jnp.zeros((weight_rows, block_users), jnp.float32)
                for j in range(items_dev + 1):
                    w = weights[d, j, pl.ds(i, 1), :]
                    extra = jnp.where(extra_row == j, w, extra)
                    if j < items_dev:
                        left.append(turned * jnp.broadcast_to(w, turned.shape).astype(jnp.bfloat16))
                left.append(extra.astype(jnp.bfloat16))
                lefts.append(jnp.concatenate(left, axis=0))
                rights.append(block)
            acc[...] += jnp.dot(
                jnp.concatenate(lefts, axis=1),
                jnp.concatenate(rights, axis=0),
                preferred_element_type=jnp.float32,
            )
            return carry

        lax.fori_loop(0, capacity, slots, 0, unroll=7)

        common = plain[...]
        live_sum = acc[gram_rows + items_dev : gram_rows + items_dev + 1, :]
        for j in range(items_dev):
            owner, place = j // items_here, j % items_here
            part[owner, place, :factor_width, :] = (
                acc[j * factor_width : (j + 1) * factor_width, :] + common
            )
            part[owner, place, factor_width:, :] = jnp.broadcast_to(
                acc[gram_rows + j : gram_rows + j + 1, :] + live_sum, (8, factor_width)
            )
        for d in range(1, peer_count):
            target = lax.rem(me_user + d, peer_count)
            copy = pltpu.make_async_remote_copy(
                src_ref=part.at[target], dst_ref=part_in.at[d - 1],
                send_sem=part_send.at[d], recv_sem=part_recv.at[d],
                device_id=(me_item, target), device_id_type=MESH,
            )
            copy.start()
            sent.append(copy)
        for d in range(1, peer_count):
            pltpu.make_async_remote_copy(
                src_ref=part.at[0], dst_ref=part_in.at[d - 1],
                send_sem=part_send.at[d], recv_sem=part_recv.at[d],
                device_id=(twin, me_user), device_id_type=MESH,
            ).wait_recv()

        row_at = lax.broadcasted_iota(jnp.int32, (factor_width, factor_width), 0)
        col_at = lax.broadcasted_iota(jnp.int32, (factor_width, factor_width), 1)
        diagonal = row_at == col_at
        for place in range(items_here):
            whole = part[me_user, place]
            for d in range(1, peer_count):
                whole = whole + part_in[d - 1, place]
            system = whole[:factor_width] + jnp.where(diagonal, ridge_weight, 0.0)
            residual = whole[factor_width : factor_width + 1]
            answer = jnp.zeros_like(residual)
            direction = residual
            norm_now = jnp.sum(residual * residual, axis=1, keepdims=True)
            for _ in range(ITERS):
                image = jnp.sum(system * direction, axis=1, keepdims=True)
                image = jnp.sum(jnp.where(diagonal, image, 0.0), axis=0, keepdims=True)
                alpha = norm_now / (jnp.sum(direction * image, axis=1, keepdims=True) + small_eps)
                answer = answer + alpha * direction
                residual = residual - alpha * image
                norm_next = jnp.sum(residual * residual, axis=1, keepdims=True)
                direction = residual + norm_next / (norm_now + small_eps) * direction
                norm_now = norm_next
            out_ref[place : place + 1, :] = answer
        for copy in sent:
            copy.wait_send()

    vmem = pl.BlockSpec(memory_space=pltpu.VMEM)
    dma = pltpu.SemaphoreType.DMA
    return pl.pallas_call(
        kernel,
        out_shape=jax.ShapeDtypeStruct((items_here, factor_width), jnp.float32),
        in_specs=[vmem] * 4 + [pl.BlockSpec(memory_space=pltpu.SMEM)],
        out_specs=vmem,
        scratch_shapes=[
            pltpu.VMEM((item_count * tiles_here, 16, factor_width), jnp.bfloat16),
            pltpu.VMEM((peer_count, items_dev + 1, held, block_users), jnp.bfloat16),
            pltpu.VMEM((peer_count - 1, items_dev + 1, held, block_users), jnp.bfloat16),
            pltpu.VMEM((peer_count, items_dev + 1, held, block_users), jnp.float32),
            pltpu.VMEM((8, lanes), jnp.int32),
            pltpu.VMEM((peer_count, 8, lanes), jnp.int32),
            pltpu.SMEM((peer_count, 8, lanes), jnp.int32),
            pltpu.VMEM((gram_rows + weight_rows, factor_width), jnp.float32),
            pltpu.VMEM((factor_width, factor_width), jnp.float32),
            pltpu.VMEM((peer_count, items_here, part_rows, factor_width), jnp.float32),
            pltpu.VMEM((peer_count - 1, items_here, part_rows, factor_width), jnp.float32),
            dma((6,)), dma((6,)), dma((7,)), dma((7,)),
            dma((peer_count,)), dma((peer_count,)), dma((peer_count,)), dma((peer_count,)),
            dma((peer_count,)), dma((peer_count,)), dma((2,)),
        ],
        compiler_params=pltpu.CompilerParams(
            collective_id=0, has_side_effects=True, vmem_limit_bytes=32 * 1024 * 1024
        ),
    )


def sends_ratings(user_factors, ratings, block_owner, owner_block_position, block_count):
    rows_here, factor_width = user_factors.shape
    slot_count, items_dev, block_users = ratings.shape
    peer_count = lax.axis_size("user")
    item_count = lax.axis_size("item")
    capacity = max(2, 3 * slot_count // (2 * peer_count))
    kernel = make_kernel(
        peer_count, item_count, rows_here, slot_count, capacity, items_dev, factor_width, block_users
    )
    tiled = user_factors.reshape(rows_here // 16, 16, factor_width)
    return kernel(tiled, ratings, block_owner, owner_block_position, block_count)


def by_shape(user_factors, ratings, block_owner, owner_block_position, block_count):
    fits = user_factors.shape[0] % 16 == 0 and lax.axis_size("item") == 8
    body = sends_ratings if fits else on_device
    return body(user_factors, ratings, block_owner, owner_block_position, block_count)


def solution(mesh):
    in_specs = (
        P(("user", "item"), None),
        P("user", "item", None),
        P("item", "user"),
        P("item", "user"),
        P("item", "user"),
    )
    out_specs = P(("item", "user"), None)
    return jax.shard_map(
        by_shape, mesh=mesh, in_specs=in_specs, out_specs=out_specs, check_vma=False
    )
```

```python
import jax
import jax.numpy as jnp
from jax import lax
from jax.experimental import pallas as pl
from jax.experimental.pallas import tpu as pltpu
from jax.sharding import PartitionSpec as P

ITERS = 8
MESH = pl.DeviceIdType.MESH


ridge_weight = 0.05
small_eps = 1e-06
group_blocks = 2


def conjugate_solve(system, right_side):
    solution = jnp.zeros_like(right_side)
    residual = right_side
    direction = right_side
    norm_now = jnp.sum(residual * residual, axis=-1, keepdims=True)
    for iteration in range(ITERS):
        image = jnp.einsum("jkl,jl->jk", system, direction, precision=lax.Precision.HIGHEST)
        alpha = norm_now / (jnp.sum(direction * image, axis=-1, keepdims=True) + small_eps)
        solution = solution + alpha * direction
        residual = residual - alpha * image
        norm_next = jnp.sum(residual * residual, axis=-1, keepdims=True)
        direction = residual + norm_next / (norm_now + small_eps) * direction
        norm_now = norm_next
    return solution


def block_terms(weights, block_rows, live_count, item_count):
    block_users = block_rows.shape[1]
    factor_width = block_rows.shape[2]
    group_turns = (live_count + group_blocks - 1) // group_blocks

    def accumulate(index_in_group, carry):
        gram_part, rhs_part = carry
        leading_slot = index_in_group * group_blocks
        w_group = lax.dynamic_slice_in_dim(weights, leading_slot, group_blocks, 0)
        r_group = lax.dynamic_slice_in_dim(block_rows, leading_slot, group_blocks, 0)
        live_mask = (leading_slot + jnp.arange(group_blocks, dtype=jnp.int32) < live_count).astype(
            jnp.bfloat16
        )
        w_group = w_group * live_mask[:, None, None]
        scaled = w_group[:, :, :, None] * r_group[:, None, :, :]
        gram_part = gram_part + jnp.einsum(
            "bjuk,bul->jkl", scaled, r_group, preferred_element_type=jnp.float32
        )
        live_ones = jnp.broadcast_to(live_mask[:, None], (group_blocks, block_users))
        rhs_part = rhs_part + jnp.einsum(
            "bju,buk->jk", w_group, r_group, preferred_element_type=jnp.float32
        )
        rhs_part = (
            rhs_part
            + jnp.einsum("bu,buk->k", live_ones, r_group, preferred_element_type=jnp.float32)[
                None, :
            ]
        )
        return (gram_part, rhs_part)

    initial = (
        jnp.zeros((item_count, factor_width, factor_width), jnp.float32),
        jnp.zeros((item_count, factor_width), jnp.float32),
    )
    gram_part, rhs_part = lax.fori_loop(0, group_turns, accumulate, initial)
    return jnp.concatenate([gram_part, rhs_part[:, None, :]], axis=1)


def on_device(user_factors, ratings, block_owner, owner_block_position, block_count):
    gathered = lax.all_gather(user_factors, "item", axis=0, tiled=True)
    block_users = ratings.shape[2]
    factor_width = gathered.shape[1]
    lookup = gathered.reshape(gathered.shape[0] // block_users, block_users, factor_width)
    owners = block_owner[0]
    local_ids = owner_block_position[0]
    filled = block_count[0, 0]
    peer_count = lax.axis_size("user")
    slot_count = owners.shape[0]
    capacity = max(2, 3 * slot_count // (2 * peer_count))
    onehot = (owners[:, None] == jnp.arange(peer_count, dtype=jnp.int32)[None, :]).astype(jnp.int32)
    before = jnp.cumsum(onehot, axis=0) - onehot
    position = jnp.sum(before * onehot, axis=1)
    requests = jnp.zeros((peer_count, capacity), jnp.int32).at[owners, position].set(local_ids)
    local_gram = jnp.einsum("rk,rl->kl", gathered, gathered, preferred_element_type=jnp.float32)
    fetched = lax.all_to_all(
        lookup[lax.all_to_all(requests, "user", split_axis=0, concat_axis=0, tiled=True)],
        "user",
        split_axis=0,
        concat_axis=0,
        tiled=True,
    )
    block_rows = fetched[owners, position]
    items_here = ratings.shape[1] // peer_count
    summed = lax.psum_scatter(
        block_terms(ratings, block_rows, filled, items_here * lax.axis_size("user")),
        "user",
        scatter_dimension=0,
        tiled=True,
    )
    system = summed[:, :factor_width, :]
    right_side = summed[:, factor_width, :]
    system = system + lax.psum(local_gram, "user")[None, :, :]
    system = system + ridge_weight * jnp.eye(factor_width, dtype=jnp.float32)[None, :, :]
    return conjugate_solve(system, right_side)


def make_kernel(peer_count, item_count, rows_here, slot_count, capacity, items_dev, factor_width, block_users):
    chip_count = item_count // 2
    half_chips = chip_count // 2
    items_here = items_dev // peer_count
    order = [(d, place) for d in [*range(1, peer_count), 0] for place in range(items_here)]
    first_items = items_dev // 2
    gram_rows = first_items * factor_width
    away = (peer_count - 1) * items_here
    part_rows = factor_width + 8
    weight_rows = (items_dev + 1 + 15) // 16 * 16
    held = (capacity + 15) // 16 * 16
    lanes = peer_count * held
    tiles_here = rows_here // 16
    block_tiles = block_users // 16

    def kernel(
        factors_ref, ratings_ref, owners_far, ids_far, count_ref, out_ref,
        rows, ratings_here, owners_ref, ids_ref, weights_out, weights_in, weights, meta_out, meta_in, places, acc, acc_last, plain, part, part_in,
        chip_send, chip_recv, twin_send, twin_recv,
        weight_send, weight_recv, meta_send, meta_recv, part_send, part_recv, local_sem,
    ):
        me_item = lax.axis_index("item")
        me_user = lax.axis_index("user")
        core = lax.rem(me_item, 2)
        chip = lax.div(me_item, 2)
        chip_x = lax.rem(chip, 2)
        chip_y = lax.div(chip, 2)
        twin = chip * 2 + (1 - core)
        shifts = [(dy, dx) for dy in range(half_chips) for dx in range(2) if dy or dx]

        def chip_at(dy, dx):
            return lax.rem(chip_y + dy, half_chips) * 2 + lax.rem(chip_x + dx, 2)

        across, along, corner = chip_at(0, 1), chip_at(1, 0), chip_at(1, 1)
        first = tiles_here // 2
        moves = [
            (across, 0, across), (along, 1, along), (across, 1, across),
            (along, 0, along), (corner, 0, along), (corner, 1, across),
        ]

        def shard(index):
            return rows.at[pl.ds(index * tiles_here, tiles_here)]

        def half_of(ref, start, half):
            return ref.at[pl.ds(start + half * first, tiles_here - first if half else first)]

        def half_shard(index, half):
            return half_of(rows, index * tiles_here, half)

        own_rows = pltpu.make_async_copy(factors_ref, shard(me_item), local_sem.at[0])
        own_rows.start()
        own_ratings = pltpu.make_async_copy(ratings_ref, ratings_here, local_sem.at[2])
        own_ratings.start()
        own_slots = [
            pltpu.make_async_copy(owners_far, owners_ref, local_sem.at[3]),
            pltpu.make_async_copy(ids_far, ids_ref, local_sem.at[4]),
        ]
        for copy in own_slots:
            copy.start()
        barrier = pltpu.get_barrier_semaphore()
        for dy, dx in shifts:
            pl.semaphore_signal(
                barrier, inc=1, device_id=(chip_at(dy, dx) * 2 + core, me_user), device_id_type=MESH
            )
        pl.semaphore_signal(barrier, inc=1, device_id=(twin, me_user), device_id_type=MESH)
        for d in range(1, peer_count):
            pl.semaphore_signal(
                barrier, inc=1, device_id=(me_item, lax.rem(me_user + d, peer_count)), device_id_type=MESH
            )
        pl.semaphore_wait(barrier, len(shifts) + 1 + peer_count - 1)

        def chip_copy(n, src, owner):
            return pltpu.make_async_remote_copy(
                src_ref=src, dst_ref=half_shard(owner, moves[n][1]),
                send_sem=chip_send.at[n], recv_sem=chip_recv.at[n],
                device_id=(moves[n][2] * 2 + core, me_user), device_id_type=MESH,
            )

        def twin_copy(n, src, dst):
            return pltpu.make_async_remote_copy(
                src_ref=src, dst_ref=dst,
                send_sem=twin_send.at[n], recv_sem=twin_recv.at[n],
                device_id=(twin, me_user), device_id_type=MESH,
            )

        sent = []
        for n in range(4):
            copy = chip_copy(n, half_of(factors_ref, 0, moves[n][1]), me_item)
            copy.start()
            sent.append(copy)
        copy = twin_copy(6, factors_ref, shard(me_item))
        copy.start()
        sent.append(copy)

        for copy in own_slots:
            copy.wait()
        owners = jnp.broadcast_to(owners_ref[...], (slot_count, slot_count))
        from_slot = lax.broadcasted_iota(jnp.int32, (slot_count, slot_count), 0)
        to_slot = lax.broadcasted_iota(jnp.int32, (slot_count, slot_count), 1)
        owners_down = jnp.sum(jnp.where(from_slot == to_slot, owners, 0), axis=1, keepdims=True)
        earlier = (owners_down == owners) & (from_slot < to_slot)
        rank = jnp.sum(jnp.where(earlier, 1, 0), axis=0, keepdims=True)
        code = jnp.where(to_slot[:1] < count_ref[0, 0], owners[:1] * held + rank, -1)
        chosen = lax.broadcasted_iota(jnp.int32, (lanes, slot_count), 0) == code
        ids = jnp.broadcast_to(ids_ref[...], (lanes, slot_count))
        ids_down = jnp.sum(jnp.where(chosen, ids, 0), axis=1, keepdims=True)
        place_row = lax.broadcasted_iota(jnp.int32, (lanes, lanes), 0)
        place_col = lax.broadcasted_iota(jnp.int32, (lanes, lanes), 1)
        ids_across = jnp.sum(jnp.where(place_row == place_col, ids_down, 0), axis=0, keepdims=True)
        meta_out[...] = jnp.broadcast_to(ids_across, (8, lanes))
        meta_in[0] = meta_out[...]
        picker = jnp.where(chosen, 1.0, 0.0).astype(jnp.bfloat16)
        own_ratings.wait()
        for j in range(items_dev + 1):
            if j < items_dev:
                plane = ratings_here[:, j, :]
            else:
                plane = jnp.ones((slot_count, block_users), jnp.bfloat16)
            picked = jnp.dot(picker, plane, preferred_element_type=jnp.float32).astype(jnp.bfloat16)
            for d in range(peer_count):
                weights_out[d, j] = picked[d * held : (d + 1) * held]

        def meta_copy(d, target):
            return pltpu.make_async_remote_copy(
                src_ref=meta_out, dst_ref=meta_in.at[d],
                send_sem=meta_send.at[d], recv_sem=meta_recv.at[d],
                device_id=(me_item, target), device_id_type=MESH,
            )

        def weight_copy(d, target):
            return pltpu.make_async_remote_copy(
                src_ref=weights_out.at[target], dst_ref=weights_in.at[d - 1],
                send_sem=weight_send.at[d], recv_sem=weight_recv.at[d],
                device_id=(me_item, target), device_id_type=MESH,
            )

        for d in range(1, peer_count):
            target = lax.rem(me_user + d, peer_count)
            for copy in (meta_copy(d, target), weight_copy(d, target)):
                copy.start()
                sent.append(copy)

        def add_plain(block, opening=False):
            block = block.reshape(rows_here, factor_width)
            term = lax.dot_general(
                block, block, (((0,), (0,)), ((), ())), preferred_element_type=jnp.float32
            )
            plain[...] = term if opening else plain[...] + term

        own_rows.wait()
        add_plain(rows[pl.ds(me_item * tiles_here, tiles_here)], True)
        acc[...] = jnp.zeros_like(acc)
        acc_last[...] = jnp.zeros_like(acc_last)

        def add_shard(index):
            add_plain(rows[pl.ds(index * tiles_here, tiles_here)])

        def arrived(n):
            piece = half_shard(moves[n][0] * 2 + core, moves[n][1])
            chip_copy(n, piece, moves[n][0] * 2 + core).wait_recv()
            if n < 2:
                onward = chip_copy(n + 4, piece, moves[n][0] * 2 + core)
                onward.start()
                sent.append(onward)
            handed = twin_copy(n, piece, piece)
            handed.start()
            sent.append(handed)

        def twin_arrived(n):
            piece = half_shard(moves[n][0] * 2 + 1 - core, moves[n][1])
            twin_copy(n, piece, piece).wait_recv()

        arrived(0)
        arrived(1)
        twin_copy(6, factors_ref, shard(twin)).wait_recv()
        add_shard(twin)
        arrived(2)
        arrived(3)
        add_shard(across * 2 + core)
        add_shard(along * 2 + core)
        for d in range(1, peer_count):
            meta_copy(d, lax.rem(me_user + d, peer_count)).wait_recv()
        to_scalar = pltpu.make_async_copy(meta_in, places, local_sem.at[1])
        to_scalar.start()
        weights[0] = weights_out[me_user].astype(jnp.float32)
        for d in range(1, peer_count):
            weight_copy(d, lax.rem(me_user + d, peer_count)).wait_recv()
            weights[d] = weights_in[d - 1].astype(jnp.float32)
        arrived(4)
        arrived(5)
        for n in range(4):
            twin_arrived(n)
        add_shard(across * 2 + 1 - core)
        add_shard(along * 2 + 1 - core)
        add_shard(corner * 2 + core)
        to_scalar.wait()
        twin_arrived(4)
        twin_arrived(5)
        add_shard(corner * 2 + 1 - core)

        extra_row = lax.broadcasted_iota(jnp.int32, (weight_rows, block_users), 0)

        items = [lax.rem(me_user + d, peer_count) * items_here + place for d, place in order]

        def add_slots(total, members, with_sides):
            def slots(i, carry):
                lefts, rights = [], []
                for d in range(peer_count):
                    block = rows[pl.ds(places[d, 0, me_user * held + i] * block_tiles, block_tiles)]
                    block = block.reshape(block_users, factor_width)
                    turned = block.T
                    left = []
                    extra = jnp.zeros((weight_rows, block_users), jnp.float32)
                    for n, item in enumerate(items):
                        if n in members or with_sides:
                            w = weights[d, item, pl.ds(i, 1), :]
                            extra = jnp.where(extra_row == n, w, extra)
                        if n in members:
                            left.append(turned * jnp.broadcast_to(w, turned.shape).astype(jnp.bfloat16))
                    if with_sides:
                        live = weights[d, items_dev, pl.ds(i, 1), :]
                        extra = jnp.where(extra_row == items_dev, live, extra)
                        left.append(extra.astype(jnp.bfloat16))
                    lefts.append(jnp.concatenate(left, axis=0))
                    rights.append(block)
                total[...] += jnp.dot(
                    jnp.concatenate(lefts, axis=1),
                    jnp.concatenate(rights, axis=0),
                    preferred_element_type=jnp.float32,
                )
                return carry

            lax.fori_loop(0, capacity, slots, 0, unroll=7 if capacity % 7 == 0 else 1)

        def part_copy(n):
            target = lax.rem(me_user + order[n][0], peer_count)
            return pltpu.make_async_remote_copy(
                src_ref=part.at[n], dst_ref=part_in.at[n],
                send_sem=part_send.at[n], recv_sem=part_recv.at[n],
                device_id=(me_item, target), device_id_type=MESH,
            )

        def finish(total, members):
            live_sum = acc[gram_rows + items_dev : gram_rows + items_dev + 1, :]
            for at, n in enumerate(members):
                part[n, :factor_width, :] = (
                    total[at * factor_width : (at + 1) * factor_width, :] + plain[...]
                )
                part[n, factor_width:, :] = jnp.broadcast_to(
                    acc[gram_rows + n : gram_rows + n + 1, :] + live_sum, (8, factor_width)
                )
                if n < away:
                    copy = part_copy(n)
                    copy.start()
                    sent.append(copy)

        add_slots(acc, range(first_items), True)
        finish(acc, range(first_items))
        add_slots(acc_last, range(first_items, items_dev), False)
        finish(acc_last, range(first_items, items_dev))
        for n in range(away):
            part_copy(n).wait_recv()

        row_at = lax.broadcasted_iota(jnp.int32, (factor_width, factor_width), 0)
        col_at = lax.broadcasted_iota(jnp.int32, (factor_width, factor_width), 1)
        diagonal = row_at == col_at
        for place in range(items_here):
            whole = part[away + place]
            for d in range(1, peer_count):
                whole = whole + part_in[(d - 1) * items_here + place]
            system = whole[:factor_width] + jnp.where(diagonal, ridge_weight, 0.0)
            residual = whole[factor_width : factor_width + 1]
            answer = jnp.zeros_like(residual)
            direction = residual
            norm_now = jnp.sum(residual * residual, axis=1, keepdims=True)
            for _ in range(ITERS):
                image = jnp.sum(system * direction, axis=1, keepdims=True)
                image = jnp.sum(jnp.where(diagonal, image, 0.0), axis=0, keepdims=True)
                alpha = norm_now / (jnp.sum(direction * image, axis=1, keepdims=True) + small_eps)
                answer = answer + alpha * direction
                residual = residual - alpha * image
                norm_next = jnp.sum(residual * residual, axis=1, keepdims=True)
                direction = residual + norm_next / (norm_now + small_eps) * direction
                norm_now = norm_next
            out_ref[place : place + 1, :] = answer
        for copy in sent:
            copy.wait_send()

    vmem = pl.BlockSpec(memory_space=pltpu.VMEM)
    far = pl.BlockSpec(memory_space=pltpu.HBM)
    dma = pltpu.SemaphoreType.DMA
    return pl.pallas_call(
        kernel,
        out_shape=jax.ShapeDtypeStruct((items_here, factor_width), jnp.float32),
        in_specs=[far] * 4 + [pl.BlockSpec(memory_space=pltpu.SMEM)],
        out_specs=vmem,
        scratch_shapes=[
            pltpu.VMEM((item_count * tiles_here, 16, factor_width), jnp.bfloat16),
            pltpu.VMEM((slot_count, items_dev, block_users), jnp.bfloat16),
            pltpu.VMEM((1, slot_count), jnp.int32),
            pltpu.VMEM((1, slot_count), jnp.int32),
            pltpu.VMEM((peer_count, items_dev + 1, held, block_users), jnp.bfloat16),
            pltpu.VMEM((peer_count - 1, items_dev + 1, held, block_users), jnp.bfloat16),
            pltpu.VMEM((peer_count, items_dev + 1, held, block_users), jnp.float32),
            pltpu.VMEM((8, lanes), jnp.int32),
            pltpu.VMEM((peer_count, 8, lanes), jnp.int32),
            pltpu.SMEM((peer_count, 8, lanes), jnp.int32),
            pltpu.VMEM((gram_rows + weight_rows, factor_width), jnp.float32),
            pltpu.VMEM(((items_dev - first_items) * factor_width, factor_width), jnp.float32),
            pltpu.VMEM((factor_width, factor_width), jnp.float32),
            pltpu.VMEM((items_dev, part_rows, factor_width), jnp.float32),
            pltpu.VMEM((away, part_rows, factor_width), jnp.float32),
            dma((6,)), dma((6,)), dma((7,)), dma((7,)),
            dma((peer_count,)), dma((peer_count,)), dma((peer_count,)), dma((peer_count,)),
            dma((away,)), dma((away,)), dma((5,)),
        ],
        compiler_params=pltpu.CompilerParams(
            collective_id=0, has_side_effects=True, vmem_limit_bytes=63 * 1024 * 1024
        ),
    )


def sends_ratings(user_factors, ratings, block_owner, owner_block_position, block_count):
    rows_here, factor_width = user_factors.shape
    slot_count, items_dev, block_users = ratings.shape
    peer_count = lax.axis_size("user")
    item_count = lax.axis_size("item")
    capacity = max(2, 3 * slot_count // (2 * peer_count))
    kernel = make_kernel(
        peer_count, item_count, rows_here, slot_count, capacity, items_dev, factor_width, block_users
    )
    tiled = user_factors.reshape(rows_here // 16, 16, factor_width)
    return kernel(tiled, ratings, block_owner, owner_block_position, block_count)


def by_shape(user_factors, ratings, block_owner, owner_block_position, block_count):
    fits = user_factors.shape[0] % 16 == 0 and lax.axis_size("item") == 8
    body = sends_ratings if fits else on_device
    return body(user_factors, ratings, block_owner, owner_block_position, block_count)


def solution(mesh):
    in_specs = (
        P(("user", "item"), None),
        P("user", "item", None),
        P("item", "user"),
        P("item", "user"),
        P("item", "user"),
    )
    out_specs = P(("item", "user"), None)
    return jax.shard_map(
        by_shape, mesh=mesh, in_specs=in_specs, out_specs=out_specs, check_vma=False
    )
```

```python
import jax
import jax.numpy as jnp
from jax import lax
from jax.experimental import pallas as pl
from jax.experimental.pallas import tpu as pltpu
from jax.sharding import PartitionSpec as P

ITERS = 8
MESH = pl.DeviceIdType.MESH


ridge_weight = 0.05
small_eps = 1e-06
group_blocks = 2


def conjugate_solve(system, right_side):
    solution = jnp.zeros_like(right_side)
    residual = right_side
    direction = right_side
    norm_now = jnp.sum(residual * residual, axis=-1, keepdims=True)
    for iteration in range(ITERS):
        image = jnp.einsum("jkl,jl->jk", system, direction, precision=lax.Precision.HIGHEST)
        alpha = norm_now / (jnp.sum(direction * image, axis=-1, keepdims=True) + small_eps)
        solution = solution + alpha * direction
        residual = residual - alpha * image
        norm_next = jnp.sum(residual * residual, axis=-1, keepdims=True)
        direction = residual + norm_next / (norm_now + small_eps) * direction
        norm_now = norm_next
    return solution


def block_terms(weights, block_rows, live_count, item_count):
    block_users = block_rows.shape[1]
    factor_width = block_rows.shape[2]
    group_turns = (live_count + group_blocks - 1) // group_blocks

    def accumulate(index_in_group, carry):
        gram_part, rhs_part = carry
        leading_slot = index_in_group * group_blocks
        w_group = lax.dynamic_slice_in_dim(weights, leading_slot, group_blocks, 0)
        r_group = lax.dynamic_slice_in_dim(block_rows, leading_slot, group_blocks, 0)
        live_mask = (leading_slot + jnp.arange(group_blocks, dtype=jnp.int32) < live_count).astype(
            jnp.bfloat16
        )
        w_group = w_group * live_mask[:, None, None]
        scaled = w_group[:, :, :, None] * r_group[:, None, :, :]
        gram_part = gram_part + jnp.einsum(
            "bjuk,bul->jkl", scaled, r_group, preferred_element_type=jnp.float32
        )
        live_ones = jnp.broadcast_to(live_mask[:, None], (group_blocks, block_users))
        rhs_part = rhs_part + jnp.einsum(
            "bju,buk->jk", w_group, r_group, preferred_element_type=jnp.float32
        )
        rhs_part = (
            rhs_part
            + jnp.einsum("bu,buk->k", live_ones, r_group, preferred_element_type=jnp.float32)[
                None, :
            ]
        )
        return (gram_part, rhs_part)

    initial = (
        jnp.zeros((item_count, factor_width, factor_width), jnp.float32),
        jnp.zeros((item_count, factor_width), jnp.float32),
    )
    gram_part, rhs_part = lax.fori_loop(0, group_turns, accumulate, initial)
    return jnp.concatenate([gram_part, rhs_part[:, None, :]], axis=1)


def on_device(user_factors, ratings, block_owner, owner_block_position, block_count):
    gathered = lax.all_gather(user_factors, "item", axis=0, tiled=True)
    block_users = ratings.shape[2]
    factor_width = gathered.shape[1]
    lookup = gathered.reshape(gathered.shape[0] // block_users, block_users, factor_width)
    owners = block_owner[0]
    local_ids = owner_block_position[0]
    filled = block_count[0, 0]
    peer_count = lax.axis_size("user")
    slot_count = owners.shape[0]
    capacity = max(2, 3 * slot_count // (2 * peer_count))
    onehot = (owners[:, None] == jnp.arange(peer_count, dtype=jnp.int32)[None, :]).astype(jnp.int32)
    before = jnp.cumsum(onehot, axis=0) - onehot
    position = jnp.sum(before * onehot, axis=1)
    requests = jnp.zeros((peer_count, capacity), jnp.int32).at[owners, position].set(local_ids)
    local_gram = jnp.einsum("rk,rl->kl", gathered, gathered, preferred_element_type=jnp.float32)
    fetched = lax.all_to_all(
        lookup[lax.all_to_all(requests, "user", split_axis=0, concat_axis=0, tiled=True)],
        "user",
        split_axis=0,
        concat_axis=0,
        tiled=True,
    )
    block_rows = fetched[owners, position]
    items_here = ratings.shape[1] // peer_count
    summed = lax.psum_scatter(
        block_terms(ratings, block_rows, filled, items_here * lax.axis_size("user")),
        "user",
        scatter_dimension=0,
        tiled=True,
    )
    system = summed[:, :factor_width, :]
    right_side = summed[:, factor_width, :]
    system = system + lax.psum(local_gram, "user")[None, :, :]
    system = system + ridge_weight * jnp.eye(factor_width, dtype=jnp.float32)[None, :, :]
    return conjugate_solve(system, right_side)


def make_kernel(peer_count, item_count, rows_here, slot_count, capacity, items_dev, factor_width, block_users):
    chip_count = item_count // 2
    half_chips = chip_count // 2
    items_here = items_dev // peer_count
    order = [(d, place) for d in [*range(1, peer_count), 0] for place in range(items_here)]
    first_items = items_dev // 2
    gram_rows = first_items * factor_width
    away = (peer_count - 1) * items_here
    part_rows = factor_width + 8
    weight_rows = (items_dev + 1 + 15) // 16 * 16
    held = (capacity + 15) // 16 * 16
    lanes = peer_count * held
    tiles_here = rows_here // 16
    block_tiles = block_users // 16

    def kernel(
        factors_ref, ratings_ref, owners_far, ids_far, count_ref, out_ref,
        rows, ratings_here, owners_ref, ids_ref, weights_out, weights_in, weights, meta_out, meta_in, places, acc, acc_last, plain, part, part_in,
        chip_send, chip_recv, twin_send, twin_recv,
        weight_send, weight_recv, meta_send, meta_recv, part_send, part_recv, local_sem,
    ):
        me_item = lax.axis_index("item")
        me_user = lax.axis_index("user")
        core = lax.rem(me_item, 2)
        chip = lax.div(me_item, 2)
        chip_x = lax.rem(chip, 2)
        chip_y = lax.div(chip, 2)
        twin = chip * 2 + (1 - core)
        shifts = [(dy, dx) for dy in range(half_chips) for dx in range(2) if dy or dx]

        def chip_at(dy, dx):
            return lax.rem(chip_y + dy, half_chips) * 2 + lax.rem(chip_x + dx, 2)

        across, along, corner = chip_at(0, 1), chip_at(1, 0), chip_at(1, 1)
        first = tiles_here // 2
        moves = [
            (across, 0, across), (along, 1, along), (across, 1, across),
            (along, 0, along), (corner, 0, along), (corner, 1, across),
        ]

        def shard(index):
            return rows.at[pl.ds(index * tiles_here, tiles_here)]

        def half_of(ref, start, half):
            return ref.at[pl.ds(start + half * first, tiles_here - first if half else first)]

        def half_shard(index, half):
            return half_of(rows, index * tiles_here, half)

        own_rows = pltpu.make_async_copy(factors_ref, shard(me_item), local_sem.at[0])
        own_rows.start()
        own_ratings = pltpu.make_async_copy(ratings_ref, ratings_here, local_sem.at[2])
        own_ratings.start()
        own_slots = [
            pltpu.make_async_copy(owners_far, owners_ref, local_sem.at[3]),
            pltpu.make_async_copy(ids_far, ids_ref, local_sem.at[4]),
        ]
        for copy in own_slots:
            copy.start()
        barrier = pltpu.get_barrier_semaphore()
        for dy, dx in shifts:
            pl.semaphore_signal(
                barrier, inc=1, device_id=(chip_at(dy, dx) * 2 + core, me_user), device_id_type=MESH
            )
        pl.semaphore_signal(barrier, inc=1, device_id=(twin, me_user), device_id_type=MESH)
        for d in range(1, peer_count):
            pl.semaphore_signal(
                barrier, inc=1, device_id=(me_item, lax.rem(me_user + d, peer_count)), device_id_type=MESH
            )
        pl.semaphore_wait(barrier, len(shifts) + 1 + peer_count - 1)

        def chip_copy(n, src, owner):
            return pltpu.make_async_remote_copy(
                src_ref=src, dst_ref=half_shard(owner, moves[n][1]),
                send_sem=chip_send.at[n], recv_sem=chip_recv.at[n],
                device_id=(moves[n][2] * 2 + core, me_user), device_id_type=MESH,
            )

        def twin_copy(n, src, dst):
            return pltpu.make_async_remote_copy(
                src_ref=src, dst_ref=dst,
                send_sem=twin_send.at[n], recv_sem=twin_recv.at[n],
                device_id=(twin, me_user), device_id_type=MESH,
            )

        sent = []
        for n in range(4):
            copy = chip_copy(n, half_of(factors_ref, 0, moves[n][1]), me_item)
            copy.start()
            sent.append(copy)
        copy = twin_copy(6, factors_ref, shard(me_item))
        copy.start()
        sent.append(copy)

        for copy in own_slots:
            copy.wait()
        owners = jnp.broadcast_to(owners_ref[...], (slot_count, slot_count))
        from_slot = lax.broadcasted_iota(jnp.int32, (slot_count, slot_count), 0)
        to_slot = lax.broadcasted_iota(jnp.int32, (slot_count, slot_count), 1)
        owners_down = jnp.sum(jnp.where(from_slot == to_slot, owners, 0), axis=1, keepdims=True)
        earlier = (owners_down == owners) & (from_slot < to_slot)
        rank = jnp.sum(jnp.where(earlier, 1, 0), axis=0, keepdims=True)
        code = jnp.where(to_slot[:1] < count_ref[0, 0], owners[:1] * held + rank, -1)
        chosen = lax.broadcasted_iota(jnp.int32, (lanes, slot_count), 0) == code
        ids = jnp.broadcast_to(ids_ref[...], (lanes, slot_count))
        ids_down = jnp.sum(jnp.where(chosen, ids, 0), axis=1, keepdims=True)
        place_row = lax.broadcasted_iota(jnp.int32, (lanes, lanes), 0)
        place_col = lax.broadcasted_iota(jnp.int32, (lanes, lanes), 1)
        ids_across = jnp.sum(jnp.where(place_row == place_col, ids_down, 0), axis=0, keepdims=True)
        meta_out[...] = jnp.broadcast_to(ids_across, (8, lanes))
        meta_in[0] = meta_out[...]
        picker = jnp.where(chosen, 1.0, 0.0).astype(jnp.bfloat16)
        own_ratings.wait()
        for j in range(items_dev + 1):
            if j < items_dev:
                plane = ratings_here[:, j, :]
            else:
                plane = jnp.ones((slot_count, block_users), jnp.bfloat16)
            picked = jnp.dot(picker, plane, preferred_element_type=jnp.float32).astype(jnp.bfloat16)
            for d in range(peer_count):
                weights_out[d, j] = picked[d * held : (d + 1) * held]

        def meta_copy(d, target):
            return pltpu.make_async_remote_copy(
                src_ref=meta_out, dst_ref=meta_in.at[d],
                send_sem=meta_send.at[d], recv_sem=meta_recv.at[d],
                device_id=(me_item, target), device_id_type=MESH,
            )

        def weight_copy(d, target):
            return pltpu.make_async_remote_copy(
                src_ref=weights_out.at[target], dst_ref=weights_in.at[d - 1],
                send_sem=weight_send.at[d], recv_sem=weight_recv.at[d],
                device_id=(me_item, target), device_id_type=MESH,
            )

        for d in range(1, peer_count):
            target = lax.rem(me_user + d, peer_count)
            for copy in (meta_copy(d, target), weight_copy(d, target)):
                copy.start()
                sent.append(copy)

        def add_plain(block, opening=False):
            block = block.reshape(rows_here, factor_width)
            term = lax.dot_general(
                block, block, (((0,), (0,)), ((), ())), preferred_element_type=jnp.float32
            )
            plain[...] = term if opening else plain[...] + term

        own_rows.wait()
        add_plain(rows[pl.ds(me_item * tiles_here, tiles_here)], True)
        acc[...] = jnp.zeros_like(acc)
        acc_last[...] = jnp.zeros_like(acc_last)

        def add_shard(index):
            add_plain(rows[pl.ds(index * tiles_here, tiles_here)])

        def arrived(n):
            piece = half_shard(moves[n][0] * 2 + core, moves[n][1])
            chip_copy(n, piece, moves[n][0] * 2 + core).wait_recv()
            if n < 2:
                onward = chip_copy(n + 4, piece, moves[n][0] * 2 + core)
                onward.start()
                sent.append(onward)
            handed = twin_copy(n, piece, piece)
            handed.start()
            sent.append(handed)

        def twin_arrived(n):
            piece = half_shard(moves[n][0] * 2 + 1 - core, moves[n][1])
            twin_copy(n, piece, piece).wait_recv()

        arrived(0)
        arrived(1)
        twin_copy(6, factors_ref, shard(twin)).wait_recv()
        add_shard(twin)
        arrived(2)
        arrived(3)
        add_shard(across * 2 + core)
        add_shard(along * 2 + core)
        for d in range(1, peer_count):
            meta_copy(d, lax.rem(me_user + d, peer_count)).wait_recv()
        to_scalar = pltpu.make_async_copy(meta_in, places, local_sem.at[1])
        to_scalar.start()
        weights[0] = weights_out[me_user].astype(jnp.float32)
        for d in range(1, peer_count):
            weight_copy(d, lax.rem(me_user + d, peer_count)).wait_recv()
            weights[d] = weights_in[d - 1].astype(jnp.float32)
        arrived(4)
        arrived(5)
        for n in range(4):
            twin_arrived(n)
        add_shard(across * 2 + 1 - core)
        add_shard(along * 2 + 1 - core)
        add_shard(corner * 2 + core)
        to_scalar.wait()
        twin_arrived(4)
        twin_arrived(5)
        add_shard(corner * 2 + 1 - core)

        extra_row = lax.broadcasted_iota(jnp.int32, (weight_rows, block_users), 0)

        items = [lax.rem(me_user + d, peer_count) * items_here + place for d, place in order]

        def add_slots(total, members, with_sides):
            def slots(i, carry):
                lefts, rights = [], []
                for d in range(peer_count):
                    block = rows[pl.ds(places[d, 0, me_user * held + i] * block_tiles, block_tiles)]
                    block = block.reshape(block_users, factor_width)
                    turned = block.T
                    left = []
                    extra = jnp.zeros((weight_rows, block_users), jnp.float32)
                    for n, item in enumerate(items):
                        if n in members or with_sides:
                            w = weights[d, item, pl.ds(i, 1), :]
                            extra = jnp.where(extra_row == n, w, extra)
                        if n in members:
                            left.append(turned * jnp.broadcast_to(w, turned.shape).astype(jnp.bfloat16))
                    if with_sides:
                        live = weights[d, items_dev, pl.ds(i, 1), :]
                        extra = jnp.where(extra_row == items_dev, live, extra)
                        left.append(extra.astype(jnp.bfloat16))
                    lefts.append(jnp.concatenate(left, axis=0))
                    rights.append(block)
                total[...] += jnp.dot(
                    jnp.concatenate(lefts, axis=1),
                    jnp.concatenate(rights, axis=0),
                    preferred_element_type=jnp.float32,
                )
                return carry

            lax.fori_loop(0, capacity, slots, 0, unroll=7 if capacity % 7 == 0 else 1)

        def part_copy(n):
            target = lax.rem(me_user + order[n][0], peer_count)
            return pltpu.make_async_remote_copy(
                src_ref=part.at[n], dst_ref=part_in.at[n],
                send_sem=part_send.at[n], recv_sem=part_recv.at[n],
                device_id=(me_item, target), device_id_type=MESH,
            )

        def finish(total, members):
            live_sum = acc[gram_rows + items_dev : gram_rows + items_dev + 1, :]
            for at, n in enumerate(members):
                part[n, :factor_width, :] = (
                    total[at * factor_width : (at + 1) * factor_width, :] + plain[...]
                )
                part[n, factor_width:, :] = jnp.broadcast_to(
                    acc[gram_rows + n : gram_rows + n + 1, :] + live_sum, (8, factor_width)
                )
                if n < away:
                    copy = part_copy(n)
                    copy.start()
                    sent.append(copy)

        add_slots(acc, range(first_items), True)
        finish(acc, range(first_items))
        add_slots(acc_last, range(first_items, items_dev), False)
        finish(acc_last, range(first_items, items_dev))
        for n in range(away):
            part_copy(n).wait_recv()

        row_at = lax.broadcasted_iota(jnp.int32, (factor_width, factor_width), 0)
        col_at = lax.broadcasted_iota(jnp.int32, (factor_width, factor_width), 1)
        diagonal = row_at == col_at
        for place in range(items_here):
            whole = part[away + place]
            for d in range(1, peer_count):
                whole = whole + part_in[(d - 1) * items_here + place]
            system = whole[:factor_width] + jnp.where(diagonal, ridge_weight, 0.0)
            residual = whole[factor_width : factor_width + 1]
            answer = jnp.zeros_like(residual)
            direction = residual

            def down(square):
                return jnp.broadcast_to(jnp.sum(square, axis=1, keepdims=True), square.shape)

            residual_down = down(jnp.where(diagonal, residual, 0.0))
            direction_down = residual_down
            norm_now = jnp.sum(residual_down * residual_down, axis=0, keepdims=True)
            for _ in range(ITERS):
                image_down = down(system * direction)
                image = jnp.sum(jnp.where(diagonal, image_down, 0.0), axis=0, keepdims=True)
                curve = jnp.sum(direction_down * image_down, axis=0, keepdims=True)
                alpha = norm_now / (curve + small_eps)
                answer = answer + alpha * direction
                residual = residual - alpha * image
                residual_down = residual_down - alpha * image_down
                norm_next = jnp.sum(residual_down * residual_down, axis=0, keepdims=True)
                beta = norm_next / (norm_now + small_eps)
                direction = residual + beta * direction
                direction_down = residual_down + beta * direction_down
                norm_now = norm_next
            out_ref[place : place + 1, :] = answer
        for copy in sent:
            copy.wait_send()

    vmem = pl.BlockSpec(memory_space=pltpu.VMEM)
    far = pl.BlockSpec(memory_space=pltpu.HBM)
    dma = pltpu.SemaphoreType.DMA
    return pl.pallas_call(
        kernel,
        out_shape=jax.ShapeDtypeStruct((items_here, factor_width), jnp.float32),
        in_specs=[far] * 4 + [pl.BlockSpec(memory_space=pltpu.SMEM)],
        out_specs=vmem,
        scratch_shapes=[
            pltpu.VMEM((item_count * tiles_here, 16, factor_width), jnp.bfloat16),
            pltpu.VMEM((slot_count, items_dev, block_users), jnp.bfloat16),
            pltpu.VMEM((1, slot_count), jnp.int32),
            pltpu.VMEM((1, slot_count), jnp.int32),
            pltpu.VMEM((peer_count, items_dev + 1, held, block_users), jnp.bfloat16),
            pltpu.VMEM((peer_count - 1, items_dev + 1, held, block_users), jnp.bfloat16),
            pltpu.VMEM((peer_count, items_dev + 1, held, block_users), jnp.float32),
            pltpu.VMEM((8, lanes), jnp.int32),
            pltpu.VMEM((peer_count, 8, lanes), jnp.int32),
            pltpu.SMEM((peer_count, 8, lanes), jnp.int32),
            pltpu.VMEM((gram_rows + weight_rows, factor_width), jnp.float32),
            pltpu.VMEM(((items_dev - first_items) * factor_width, factor_width), jnp.float32),
            pltpu.VMEM((factor_width, factor_width), jnp.float32),
            pltpu.VMEM((items_dev, part_rows, factor_width), jnp.float32),
            pltpu.VMEM((away, part_rows, factor_width), jnp.float32),
            dma((6,)), dma((6,)), dma((7,)), dma((7,)),
            dma((peer_count,)), dma((peer_count,)), dma((peer_count,)), dma((peer_count,)),
            dma((away,)), dma((away,)), dma((5,)),
        ],
        compiler_params=pltpu.CompilerParams(
            collective_id=0, has_side_effects=True, vmem_limit_bytes=63 * 1024 * 1024
        ),
    )


def sends_ratings(user_factors, ratings, block_owner, owner_block_position, block_count):
    rows_here, factor_width = user_factors.shape
    slot_count, items_dev, block_users = ratings.shape
    peer_count = lax.axis_size("user")
    item_count = lax.axis_size("item")
    capacity = max(2, 3 * slot_count // (2 * peer_count))
    kernel = make_kernel(
        peer_count, item_count, rows_here, slot_count, capacity, items_dev, factor_width, block_users
    )
    tiled = user_factors.reshape(rows_here // 16, 16, factor_width)
    return kernel(tiled, ratings, block_owner, owner_block_position, block_count)


def by_shape(user_factors, ratings, block_owner, owner_block_position, block_count):
    fits = user_factors.shape[0] % 16 == 0 and lax.axis_size("item") == 8
    body = sends_ratings if fits else on_device
    return body(user_factors, ratings, block_owner, owner_block_position, block_count)


def solution(mesh):
    in_specs = (
        P(("user", "item"), None),
        P("user", "item", None),
        P("item", "user"),
        P("item", "user"),
        P("item", "user"),
    )
    out_specs = P(("item", "user"), None)
    return jax.shard_map(
        by_shape, mesh=mesh, in_specs=in_specs, out_specs=out_specs, check_vma=False
    )
```
